256 devices in a mesh: gx: 32 (over x, z_hi, core), gy: 8 (over y, z_lo).
Axes of the slice: x: 4, y: 4, z: 8 (z_hi: 4, z_lo: 2; z = z_hi * 2 + z_lo), core: 2. Of those that a mesh axis runs over, the one named last changes fastest.
Arguments:
- populations: float32 [19, 256, 128, 128], P(None, 'gx', 'gy'), may hold values from 0.0097 to 0.5, as said below
- cell_flags: int32 [4, 256, 128, 128], P(None, 'gx', 'gy'), may hold values from 0 to 3, as said below
- fill_level: float32 [256, 128, 128], P('gx', 'gy'), may hold values from 0.05 to 0.95
- tile_block: int32 [64, 8], P('gx', 'gy'), may hold values from 0 to 255, as said below
- deck_weights: bfloat16 [64, 8, 64, 1024], P('gx', 'gy'), may hold values from -1.5 to 1.5
Outputs:
- final_populations: float32 [19, 256, 128, 128], P(None, 'gx', 'gy')
- mass_change: float32 [256, 128, 128], P('gx', 'gy')
- shell_loads: float32 [256, 4, 1024], P(('gx', 'gy'))
The draws below stay inside these ranges and needn't reach their ends.
Inputs may be any that keep to these rules, and one draw needn't show every extreme that they name: `cell_flags`: 0 fluid, 1 interface, 2 gas, 3 wall. `tile_block`: every block is named by exactly 2 tiles. `populations`: each population is its lattice weight times a factor between 0.35 and 1.65.
All inputs are finite; a program needn't handle non-finite values.
Results may differ from the reference program's by a relative error of at most 0.0029.
Values sent between devices are 32-bit elements; how exact they have to be, the bound alone decides.
A program may use at most 192 MiB of HBM per device.

```python
import jax
import jax.numpy as jnp
from jax import lax

CY = 16
NZ = 128
STEPS = 4
BSZ = 1024
NX = 256
NY = 128
BLOCKS = 256
N_GX = 32
N_GY = 8


def draw_populations(key, part):
    key = jax.random.fold_in(key, 3)
    lattice = jnp.array([1.0 / 3.0] + [1.0 / 18.0] * 6 + [1.0 / 36.0] * 12, jnp.float32)
    factor = 1.0 + jax.random.uniform(key, (19, NX, NY, NZ), jnp.float32, -0.5, 0.5)
    return (lattice[:, None, None, None] * factor).astype(jnp.float32)


def draw_cell_flags(key, part):
    key = jax.random.fold_in(key, 1)
    height_key, chance_key = jax.random.split(key)
    heights = jax.random.randint(height_key, (STEPS, NX, NY, 1), 0, NZ)
    levels = jnp.arange(NZ, dtype=jnp.int32)
    surface = jnp.where(levels < heights, 0, jnp.where(levels == heights, 1, 2))
    chance = jax.random.randint(chance_key, (STEPS, NX, NY, NZ), 0, 100)
    kinds = jnp.where(chance < 6, 3, jnp.where(chance < 30, 1, surface))
    return kinds.astype(jnp.int32)


def bring(order, block_id, sender):
    holder = jnp.argmax(order == block_id).astype(jnp.int32)
    displaced = order[sender]
    return order.at[holder].set(displaced).at[sender].set(block_id)


def draw_tile_block(key, part):
    key = jax.random.fold_in(key, 2)
    slots = NX // 4 // N_GX
    slot_keys = jax.random.split(key, slots + 1)
    shuffles = jax.vmap(lambda single: jax.random.permutation(single, BLOCKS))(slot_keys[:slots])
    chosen = jax.random.randint(slot_keys[slots], (), 0, BLOCKS).astype(jnp.int32)
    sender = (chosen + 1) % BLOCKS
    paired = (chosen + 2) % BLOCKS
    far_sender = (paired + BLOCKS // 2) % BLOCKS
    first = shuffles[0].astype(jnp.int32)
    first = bring(first, chosen, sender)
    first = bring(first, paired, far_sender)
    shuffles = shuffles.astype(jnp.int32).at[0].set(first)
    arranged = shuffles.reshape(slots, N_GX, N_GY).transpose(1, 0, 2).reshape(N_GX * slots, N_GY)
    return arranged.astype(jnp.int32)


def block_levels(own_key, dims, cuts, low, largest):
    def one(dim, shards_of):
        steps = jax.random.uniform(jax.random.fold_in(jax.random.fold_in(own_key, 6), dim), (shards_of,), jnp.float32, low / len(cuts), largest / len(cuts))
        return jnp.repeat(jnp.exp(steps), dims[dim] // shards_of).reshape((-1,) + (1,) * (len(dims) - dim - 1))

    factor_of = one(*cuts[0])
    for cut in cuts[1:]:
        factor_of = factor_of * one(*cut)
    return factor_of


def scatter_about(own_key, shape, scale, reach, cuts=(), held_as=jnp.bfloat16):
    level = block_levels(own_key, shape, cuts, -0.22, 0.18) if cuts else 1.0
    values = jax.random.normal(own_key, shape, jnp.float32) * scale * level
    return jnp.minimum(jnp.maximum(values, -reach), reach).astype(held_as)


def setup_inputs(seed: int = 0) -> dict:
    key_list = jax.random.split(jax.random.key(seed), 6)
    return {
        "populations": draw_populations(jax.random.fold_in(key_list[5], 71), 0),
        "cell_flags": draw_cell_flags(jax.random.fold_in(key_list[5], 71), 0),
        "fill_level": jnp.clip(0.05 + 0.9 * jax.random.uniform(key_list[2], (NX, NY, NZ), jnp.float32) ** block_levels(key_list[2], (NX, NY, NZ), ((0, 32), (1, 8)), -0.2, 0.2), 0.05, 0.95),
        "tile_block": draw_tile_block(jax.random.fold_in(key_list[5], 71), 0),
        "deck_weights": scatter_about(key_list[4], (NX // 4, N_GY, 4 * CY, BSZ), 0.25, 1.5, ((0, 32), (1, 8))),
    }


velocity_table = ((0, 0, 0), (1, 0, 0), (-1, 0, 0), (0, 1, 0), (0, -1, 0), (0, 0, 1), (0, 0, -1),
                  (1, 1, 0), (-1, -1, 0), (1, -1, 0), (-1, 1, 0), (1, 0, 1), (-1, 0, -1), (1, 0, -1),
                  (-1, 0, 1), (0, 1, 1), (0, -1, -1), (0, 1, -1), (0, -1, 1))
weight_table = (1.0 / 3.0,) + (1.0 / 18.0,) * 6 + (1.0 / 36.0,) * 12
opposite_index = (0, 2, 1, 4, 3, 6, 5, 8, 7, 10, 9, 12, 11, 14, 13, 16, 15, 18, 17)
relax_time = 0.8
gravity = 0.001


def project_onto(component, vector):
    result = None
    for dimension in range(3):
        factor = velocity_table[component][dimension]
        if factor != 0:
            addend = float(factor) * vector[dimension]
            result = addend if result is None else result + addend
    return result


def momentum(values_in):
    totals = []
    for dimension in range(3):
        summed = None
        for component in range(19):
            factor = velocity_table[component][dimension]
            if factor != 0:
                addend = float(factor) * values_in[component]
                summed = addend if summed is None else summed + addend
        totals.append(summed)
    return totals


def phase_of(cell_flag, fill_level):
    return jnp.where(cell_flag == 0, 1.0, jnp.where(cell_flag == 1, fill_level,
                     jnp.where(cell_flag == 2, 0.0, -1.0))).astype(jnp.float32)


def pad_depth(block):
    plane_shape = block.shape[:3] + (1,)
    below = jnp.zeros(plane_shape, jnp.float32).at[19].set(-1.0)
    above = jnp.zeros(plane_shape, jnp.float32)
    return jnp.concatenate([below, block, above], axis=3)


def advance(padded, resident, fill_level, cell_flag):
    cells_x, cells_y, cells_z = resident.shape[1], resident.shape[2], resident.shape[3]
    current = momentum(resident)
    speed_square = current[0] * current[0] + current[1] * current[1] + current[2] * current[2]
    read = [resident[0]]
    exchanged = jnp.zeros(resident.shape[1:], jnp.float32)
    for component in range(1, 19):
        shift_x, shift_y, shift_z = velocity_table[component]
        pulled = padded[component, 1 - shift_x:1 - shift_x + cells_x, 1 - shift_y:1 - shift_y + cells_y,
                        1 - shift_z:1 - shift_z + cells_z]
        nearby = padded[19, 1 - shift_x:1 - shift_x + cells_x, 1 - shift_y:1 - shift_y + cells_y,
                        1 - shift_z:1 - shift_z + cells_z]
        reverse = resident[opposite_index[component]]
        lattice_weight = weight_table[component]
        projection = project_onto(component, current)
        rebuilt = 2.0 * lattice_weight * (1.0 + 4.5 * projection * projection - 1.5 * speed_square) - reverse
        read.append(jnp.where(nearby < 0.0, reverse, jnp.where(nearby == 0.0, rebuilt, pulled)))
        weighting = jnp.where(nearby >= 1.0, 1.0, jnp.where(nearby > 0.0, 0.5 * (fill_level + nearby), 0.0))
        exchanged = exchanged + weighting * (pulled - reverse)
    liquid = cell_flag <= 1
    exchanged = jnp.where(cell_flag == 1, exchanged, 0.0)
    density = read[0]
    for component in range(1, 19):
        density = density + read[component]
    velocity = momentum(read)
    velocity[2] = velocity[2] - relax_time * gravity
    velocity_square = velocity[0] * velocity[0] + velocity[1] * velocity[1] + velocity[2] * velocity[2]
    relaxed = []
    for component in range(19):
        lattice_weight = weight_table[component]
        if component == 0:
            equilibrium = lattice_weight * (density - 1.5 * velocity_square)
        else:
            projection = project_onto(component, velocity)
            equilibrium = lattice_weight * (density + 3.0 * projection + 4.5 * projection * projection
                                            - 1.5 * velocity_square)
        updated = read[component] - (read[component] - equilibrium) / relax_time
        relaxed.append(jnp.where(liquid, updated, lattice_weight))
    bottom = jnp.where(liquid[:, :, 0], density[:, :, 0] / 3.0, 0.0)
    return jnp.stack(relaxed), exchanged, bottom


def reference(populations, cell_flags, fill_level, tile_block, deck_weights):
    current_pops = populations
    exchanged_total = jnp.zeros((NX, NY, NZ), jnp.float32)
    bottoms = []
    for step_index in range(STEPS):
        cell_flag = cell_flags[step_index]
        stacked = jnp.concatenate([current_pops, phase_of(cell_flag, fill_level)[None]], axis=0)
        padded = pad_depth(jnp.pad(stacked, ((0, 0), (1, 1), (1, 1), (0, 0))))

        def slab_update(slab_index, carried, padded=padded, current_pops=current_pops, cell_flag=cell_flag):
            next_state, summed_mass, bottom = carried
            offset = (slab_index * 4).astype(jnp.int32)
            window = lax.dynamic_slice_in_dim(padded, offset, 6, 1)
            resident = lax.dynamic_slice_in_dim(current_pops, offset, 4, 1)
            fill_part = lax.dynamic_slice_in_dim(fill_level, offset, 4, 0)
            flag_part = lax.dynamic_slice_in_dim(cell_flag, offset, 4, 0)
            relaxed, exchanged, bottom_row = advance(window, resident, fill_part, flag_part)
            next_state = lax.dynamic_update_slice_in_dim(next_state, relaxed, offset, 1)
            previous = lax.dynamic_slice_in_dim(summed_mass, offset, 4, 0)
            summed_mass = lax.dynamic_update_slice_in_dim(summed_mass, previous + exchanged, offset, 0)
            bottom = lax.dynamic_update_slice_in_dim(bottom, bottom_row, offset, 0)
            return next_state, summed_mass, bottom

        initial = (jnp.zeros_like(current_pops), exchanged_total, jnp.zeros((NX, NY), jnp.float32))
        current_pops, exchanged_total, bottom = lax.fori_loop(0, NX // 4, slab_update, initial)
        bottoms.append(bottom)
    deck_rows = jnp.stack(bottoms).astype(jnp.bfloat16)
    deck_tiles = deck_rows.reshape(STEPS, NX // 4, 4, N_GY, CY).transpose(0, 1, 3, 2, 4)
    deck_tiles = deck_tiles.reshape(STEPS, NX // 4, N_GY, 4 * CY)
    partials = jnp.einsum("sabc,abck->absk", deck_tiles.astype(jnp.float32), deck_weights.astype(jnp.float32),
                          precision=lax.Precision.HIGHEST)
    shell_loads = jax.ops.segment_sum(partials.reshape(-1, STEPS, BSZ), tile_block.reshape(-1),
                                      num_segments=BLOCKS)
    return current_pops, exchanged_total, shell_loads
```

```python
import functools

import jax
import jax.numpy as jnp
from jax import lax
from jax.experimental import pallas as pl
from jax.experimental.pallas import tpu as pltpu
from jax.sharding import PartitionSpec as P

velocity_table = (
    (0, 0, 0),
    (1, 0, 0),
    (-1, 0, 0),
    (0, 1, 0),
    (0, -1, 0),
    (0, 0, 1),
    (0, 0, -1),
    (1, 1, 0),
    (-1, -1, 0),
    (1, -1, 0),
    (-1, 1, 0),
    (1, 0, 1),
    (-1, 0, -1),
    (1, 0, -1),
    (-1, 0, 1),
    (0, 1, 1),
    (0, -1, -1),
    (0, 1, -1),
    (0, -1, 1),
)
weight_table = (1.0 / 3.0,) + (1.0 / 18.0,) * 6 + (1.0 / 36.0,) * 12
relax_time = 0.8
gravity = 0.001

MESH = pl.DeviceIdType.MESH
F32 = jnp.float32
STEPS = 4
CX, CY, NZ = 8, 16, 128
CELLS = CX * CY
PITCH = 24
ROWS = 248
LOW_SLAB = 8
HIGH_SLAB = PITCH * (CX + 1) + 8
X_PLUS = (1, 7, 9, 11, 13)
X_MINUS = (2, 8, 10, 12, 14)
Y_PLUS = (3, 7, 10, 15, 17)
Y_MINUS = (4, 8, 9, 16, 18)
SLOTS = X_PLUS + X_MINUS + (3, 4, 5, 6, 15, 16, 17, 18)
SLOT = {component: place for place, component in enumerate(SLOTS)}
FLUID, GAS, WALL = 1.0, -0.5, -1.0


def row_of(x, y):
    return PITCH * (x + 1) + 8 + y


def turned(block, shift):
    if shift == 0:
        return block
    return pltpu.roll(block, shift % NZ, block.ndim - 1)


def version_of(shift_z):
    return 0 if shift_z == 0 else (1 if shift_z == 1 else 2)


def dot3(direction, vector):
    result = None
    for factor, part in zip(direction, vector):
        if factor == 0:
            continue
        if result is None:
            result = part if factor > 0 else -part
        else:
            result = result + part if factor > 0 else result - part
    return result


def add_momentum(totals, direction, difference):
    for axis, factor in enumerate(direction):
        if factor == 0:
            continue
        if totals[axis] is None:
            totals[axis] = difference if factor > 0 else -difference
        elif factor > 0:
            totals[axis] = totals[axis] + difference
        else:
            totals[axis] = totals[axis] - difference


def kernel(
    gx_count,
    gy_count,
    pops_in,
    flags_in,
    fill_in,
    tile_in,
    weights_in,
    pops_out,
    mass_out,
    loads_out,
    streamed,
    resident,
    phases,
    current,
    mass,
    deck,
    flags,
    fill,
    weights_packed,
    weights,
    y_send,
    y_recv,
    corner_recv,
    hy_send,
    hy_recv,
    hcorner_recv,
    tile_send,
    tile_recv,
    index_block,
    index_scalars,
    first0,
    first1,
    first2,
    first3,
    second_send,
    second_recv,
    loads,
    local_sem,
    halo_send_sem,
    halo_recv_sem,
    route_send_sem,
    route_recv_sem,
):
    first = (first0, first1, first2, first3)
    gx = lax.axis_index("gx")
    gy = lax.axis_index("gy")
    group_count = gx_count // 2
    member_count = 2 * gy_count
    group = gx // 2
    member = lax.rem(gx, 2) * gy_count + gy
    east = lax.rem(gx + 1, gx_count)
    west = lax.rem(gx + gx_count - 1, gx_count)
    north = lax.rem(gy + 1, gy_count)
    south = lax.rem(gy + gy_count - 1, gy_count)

    def member_device(shift):
        other = lax.rem(member + shift, member_count)
        return other, (2 * group + other // gy_count, lax.rem(other, gy_count))

    def group_device(shift):
        other = lax.rem(group + shift, group_count)
        return other, (2 * other + lax.rem(gx, 2), gy)

    neighbours = (
        (east, gy),
        (west, gy),
        (gx, north),
        (gx, south),
        (east, north),
        (west, south),
        (east, south),
        (west, north),
    )

    loads_of = [
        pltpu.make_async_copy(flags_in, flags, local_sem.at[0]),
        pltpu.make_async_copy(fill_in, fill, local_sem.at[1]),
        pltpu.make_async_copy(pops_in, resident.at[0], local_sem.at[2]),
        pltpu.make_async_copy(weights_in, weights_packed, local_sem.at[3]),
    ]
    for copy in loads_of:
        copy.start()

    barrier = pltpu.get_barrier_semaphore()
    for device in neighbours:
        pl.semaphore_signal(barrier, inc=1, device_id=device, device_id_type=MESH)
    for shift in range(1, member_count):
        pl.semaphore_signal(
            barrier, inc=1, device_id=member_device(shift)[1], device_id_type=MESH
        )
    for shift in range(1, group_count):
        pl.semaphore_signal(
            barrier, inc=1, device_id=group_device(shift)[1], device_id_type=MESH
        )

    lane = lax.broadcasted_iota(jnp.int32, (8, NZ), 1)

    def put_phase(step, rows, code):
        phases[step, 0, rows, :] = code
        phases[step, 1, rows, :] = jnp.where(lane == 0, WALL, turned(code, 1))
        phases[step, 2, rows, :] = jnp.where(lane == NZ - 1, GAS, turned(code, -1))

    loads_of[0].wait()
    loads_of[1].wait()

    def code_rows(index, carry):
        x = index // 2
        half = lax.rem(index, 2)
        cells = pl.ds(pl.multiple_of(8 * index, 8), 8)
        rows = pl.ds(pl.multiple_of(PITCH * x + 32 + 8 * half, 8), 8)
        level = 0.5 * fill[cells, :]
        for step in range(STEPS):
            kind = flags[step, cells, :]
            code = jnp.where(
                kind == 0, FLUID, jnp.where(kind == 1, level, jnp.where(kind == 2, GAS, WALL))
            )
            put_phase(step, rows, code)
        return carry

    lax.fori_loop(0, 2 * CX, code_rows, 0)
    for step in range(STEPS):
        hy_send[0, step] = phases[step, 0, pl.ds(row_of(0, CY - 1), CX, stride=PITCH), :]
        hy_send[1, step] = phases[step, 0, pl.ds(row_of(0, 0), CX, stride=PITCH), :]

    loads_of[2].wait()

    def first_rows(index, carry):
        x = index // 2
        half = lax.rem(index, 2)
        cells = pl.ds(pl.multiple_of(8 * index, 8), 8)
        rows = pl.ds(pl.multiple_of(PITCH * x + 32 + 8 * half, 8), 8)
        totals = [None, None, None]
        for component in range(1, 19, 2):
            direction = velocity_table[component]
            along = resident[0, component, cells, :]
            against = resident[0, component + 1, cells, :]
            add_momentum(totals, direction, along - against)
            streamed[0, SLOT[component], rows, :] = turned(along, direction[2])
            streamed[0, SLOT[component + 1], rows, :] = turned(against, -direction[2])
        for axis in range(3):
            current[0, axis, cells, :] = totals[axis]
        return carry

    lax.fori_loop(0, 2 * CX, first_rows, 0)
    for side, (y, components) in enumerate(((CY - 1, Y_PLUS), (0, Y_MINUS))):
        for place, component in enumerate(components):
            y_send[0, side, place] = turned(
                resident[0, component, pl.ds(y, CX, stride=CY), :], velocity_table[component][2]
            )

    pl.semaphore_wait(barrier, 8 + member_count - 1 + group_count - 1)

    def remote(source, target, exchange, place, device):
        return pltpu.make_async_remote_copy(
            src_ref=source,
            dst_ref=target,
            send_sem=halo_send_sem.at[exchange, place],
            recv_sem=halo_recv_sem.at[exchange, place],
            device_id=device,
            device_id_type=MESH,
        )

    def y_copies(step):
        return [
            remote(y_send.at[step, 0], y_recv.at[step, 0], step, 2, neighbours[2]),
            remote(y_send.at[step, 1], y_recv.at[step, 1], step, 3, neighbours[3]),
            remote(y_send.at[step, 0, 1], corner_recv.at[step, 0], step, 4, neighbours[4]),
            remote(y_send.at[step, 1, 1], corner_recv.at[step, 1], step, 5, neighbours[5]),
            remote(y_send.at[step, 1, 2], corner_recv.at[step, 2], step, 6, neighbours[6]),
            remote(y_send.at[step, 0, 2], corner_recv.at[step, 3], step, 7, neighbours[7]),
        ]

    def x_copies(step):
        return [
            remote(
                streamed.at[step, pl.ds(0, 5), pl.ds(row_of(CX - 1, 0), CY), :],
                streamed.at[step, pl.ds(0, 5), pl.ds(LOW_SLAB, CY), :],
                step,
                0,
                neighbours[0],
            ),
            remote(
                streamed.at[step, pl.ds(5, 5), pl.ds(row_of(0, 0), CY), :],
                streamed.at[step, pl.ds(5, 5), pl.ds(HIGH_SLAB, CY), :],
                step,
                1,
                neighbours[1],
            ),
        ]

    phase_copies = [
        remote(
            phases.at[:, 0, pl.ds(row_of(CX - 1, 0), CY), :],
            phases.at[:, 0, pl.ds(LOW_SLAB, CY), :],
            STEPS,
            0,
            neighbours[0],
        ),
        remote(
            phases.at[:, 0, pl.ds(row_of(0, 0), CY), :],
            phases.at[:, 0, pl.ds(HIGH_SLAB, CY), :],
            STEPS,
            1,
            neighbours[1],
        ),
        remote(hy_send.at[0], hy_recv.at[0], STEPS, 2, neighbours[2]),
        remote(hy_send.at[1], hy_recv.at[1], STEPS, 3, neighbours[3]),
        remote(hy_send.at[0], hcorner_recv.at[0], STEPS, 4, neighbours[4]),
        remote(hy_send.at[1], hcorner_recv.at[1], STEPS, 5, neighbours[5]),
        remote(hy_send.at[1], hcorner_recv.at[2], STEPS, 6, neighbours[6]),
        remote(hy_send.at[0], hcorner_recv.at[3], STEPS, 7, neighbours[7]),
    ]
    halo_copies = [y_copies(step) + x_copies(step) for step in range(STEPS)]
    for copy in phase_copies:
        copy.start()
    for copy in halo_copies[0]:
        copy.start()

    tile_send[...] = jnp.where(
        lane == 2 * member,
        tile_in[0, 0],
        jnp.where(lane == 2 * member + 1, tile_in[1, 0], 0),
    )
    tile_recv[member] = tile_send[...]

    def route(source, target, kind, device):
        return pltpu.make_async_remote_copy(
            src_ref=source,
            dst_ref=target,
            send_sem=route_send_sem.at[kind],
            recv_sem=route_recv_sem.at[kind],
            device_id=device,
            device_id_type=MESH,
        )

    def wait_bytes(ref, semaphore):
        pltpu.make_async_copy(ref, ref, semaphore).wait()

    def tell_members(shift, carry):
        route(tile_send, tile_recv.at[member], 2 * STEPS, member_device(shift)[1]).start()
        return carry

    lax.fori_loop(1, member_count, tell_members, 0)

    def update(step, prow, crow, column=None):
        final = step == STEPS - 1
        pstep, cstep = (PITCH, CY) if column is not None else (None, None)

        def rows(offset):
            if pstep is None:
                return pl.ds(prow + offset, 8)
            return pl.ds(prow + offset, 8, stride=pstep)

        cells = pl.ds(crow, 8) if cstep is None else pl.ds(crow, 8, stride=cstep)
        own = phases[step, 0, rows(0), :]
        liquid = own > -0.25
        flow = [current[step, axis, cells, :] for axis in range(3)]
        flow_square = flow[0] * flow[0] + flow[1] * flow[1] + flow[2] * flow[2]
        rest = 1.0 - 1.5 * flow_square
        rest_of = {1.0 / 18.0: rest * (2.0 / 18.0), 1.0 / 36.0: rest * (2.0 / 36.0)}
        density = resident[step, 0, cells, :]
        read = [density]
        totals = [None, None, None]
        exchanged = None
        for component in range(1, 19, 2):
            direction = velocity_table[component]
            weight = weight_table[component]
            offset = PITCH * direction[0] + direction[1]
            projection = dot3(direction, flow)
            both = rest_of[weight] + (9.0 * weight) * (projection * projection)
            along = resident[step, component, cells, :]
            against = resident[step, component + 1, cells, :]
            for sign, reverse in ((1, against), (-1, along)):
                place = component if sign == 1 else component + 1
                pulled = streamed[step, SLOT[place], rows(-sign * offset), :]
                near = phases[step, version_of(sign * direction[2]), rows(-sign * offset), :]
                value = jnp.where(
                    near < -0.25, jnp.where(near < -0.75, reverse, both - reverse), pulled
                )
                share = jnp.minimum(jnp.maximum(own + near, 0.0), 1.0)
                moved = share * (pulled - reverse)
                exchanged = moved if exchanged is None else exchanged + moved
                read.append(value)
            density = density + (read[component] + read[component + 1])
            add_momentum(totals, direction, read[component] - read[component + 1])
        interface = jnp.logical_and(liquid, own < 0.75)
        exchanged = jnp.where(interface, exchanged, 0.0)
        if step > 0:
            exchanged = exchanged + mass[step - 1, cells, :]
        mass[step, cells, :] = exchanged
        deck[step, cells, :] = jnp.where(liquid, density * (1.0 / 3.0), 0.0)
        speed = [totals[0], totals[1], totals[2] - relax_time * gravity]
        speed_square = speed[0] * speed[0] + speed[1] * speed[1] + speed[2] * speed[2]
        base = density - 1.5 * speed_square
        gain = 1.0 / relax_time
        keep = 1.0 - gain

        def put(component, value):
            value = jnp.where(liquid, value, weight_table[component])
            resident[step + 1, component, cells, :] = value
            if final or component == 0:
                return
            value = turned(value, velocity_table[component][2])
            streamed[step + 1, SLOT[component], rows(0), :] = value
            if column is not None:
                side, names = (0, Y_PLUS) if column > 0 else (1, Y_MINUS)
                if component in names:
                    y_send[step + 1, side, names.index(component)] = value

        put(0, (gain * weight_table[0]) * base + keep * read[0])
        base_of = {
            1.0 / 18.0: base * (gain / 18.0),
            1.0 / 36.0: base * (gain / 36.0),
        }
        for component in range(1, 19, 2):
            weight = weight_table[component]
            projection = dot3(velocity_table[component], speed)
            even = base_of[weight] + (4.5 * gain * weight) * (projection * projection)
            odd = (3.0 * gain * weight) * projection
            put(component, (even + odd) + keep * read[component])
            put(component + 1, (even - odd) + keep * read[component + 1])
        if not final:
            after = [totals[0], totals[1], totals[2] - gravity]
            for axis in range(3):
                current[step + 1, axis, cells, :] = jnp.where(liquid, after[axis], 0.0)

    def interior(step):
        def slab(x, carry):
            for y in (1, 7):
                update(step, PITCH * x + PITCH + 8 + y, CY * x + y)
            return carry

        lax.fori_loop(1, CX - 1, slab, 0)

    def y_border(step):
        for y in (0, CY - 1):
            update(step, row_of(0, y), y, column=y)

    def x_border(step):
        def slab(index, carry):
            x = (CX - 1) * (index // 2)
            half = 8 * lax.rem(index, 2)
            update(
                step,
                pl.multiple_of(PITCH * x + PITCH + 8 + half, 8),
                pl.multiple_of(CY * x + half, 8),
            )
            return carry

        lax.fori_loop(0, 4, slab, 0)

    corners = (
        (7, row_of(-1, -1), CX - 1),
        (8, row_of(CX, CY), 0),
        (9, row_of(-1, CY), CX - 1),
        (10, row_of(CX, -1), 0),
    )

    def unpack(step):
        for copy in halo_copies[step]:
            copy.wait_recv()
        for side, (y, names) in enumerate(((-1, Y_PLUS), (CY, Y_MINUS))):
            for place, component in enumerate(names):
                streamed[step, SLOT[component], pl.ds(row_of(0, y), CX, stride=PITCH), :] = y_recv[
                    step, side, place
                ]
        for place, (component, row, x) in enumerate(corners):
            streamed[step, SLOT[component], pl.ds(row, 1), :] = corner_recv[
                step, place, pl.ds(x, 1), :
            ]

    def unpack_phases():
        for copy in phase_copies:
            copy.wait_recv()
        at_west, at_east = gx == 0, gx == gx_count - 1
        at_south, at_north = gy == 0, gy == gy_count - 1

        def one(step, carry):
            for start, edge in ((LOW_SLAB, at_west), (HIGH_SLAB, at_east)):
                for half in (0, 8):
                    rows = pl.ds(start + half, 8)
                    put_phase(step, rows, jnp.where(edge, GAS, phases[step, 0, rows, :]))
            for side, (y, edge) in enumerate(((-1, at_south), (CY, at_north))):
                rows = pl.ds(row_of(0, y), CX, stride=PITCH)
                put_phase(step, rows, jnp.where(edge, GAS, hy_recv[side, step]))
            edges = (
                at_west | at_south,
                at_east | at_north,
                at_west | at_north,
                at_east | at_south,
            )
            for place, (component, row, x) in enumerate(corners):
                code = hcorner_recv[place, step, pl.ds(x, 1), :]
                phases[step, 0, pl.ds(row, 1), :] = jnp.where(edges[place], GAS, code)
            return carry

        lax.fori_loop(0, STEPS, one, 0)

    def find_tiles():
        wait_bytes(tile_recv.at[pl.ds(0, member_count - 1)], route_recv_sem.at[2 * STEPS])
        names = tile_recv[0]
        for place in range(1, member_count):
            names = names + tile_recv[place]
        sublane = lax.broadcasted_iota(jnp.int32, (8, NZ), 0)
        none = 2 * member_count
        for part in range((group_count + 7) // 8):
            wanted = (sublane + 8 * part) * member_count + member
            match = jnp.logical_and(names == wanted, lane < none)
            last = jnp.max(jnp.where(match, lane, -1), axis=1, keepdims=True)
            early = jnp.min(jnp.where(match, lane, none), axis=1, keepdims=True)
            early = jnp.where(early == last, none, early)
            last = jnp.where(last < 0, none, last)
            index_block[0, pl.ds(8 * part, 8), :] = jnp.broadcast_to(last, (8, NZ))
            index_block[1, pl.ds(8 * part, 8), :] = jnp.broadcast_to(early, (8, NZ))
        copy = pltpu.make_async_copy(index_block, index_scalars, local_sem.at[4])
        copy.start()
        copy.wait()

    def widen_weights():
        loads_of[3].wait()
        for part in range(CELLS // 16):
            rows = pl.ds(16 * part, 16)
            weights[rows, :] = weights_packed[rows, :].astype(F32)

    def first_leg(step):
        buffer = first[step]

        def tile(place, carry):
            sums = [None] * 8
            for part in range(8):
                cells = pl.ds(pl.multiple_of(64 * place + 8 * part, 8), 8)
                pressure = deck[step, cells, :].astype(jnp.bfloat16).astype(F32)
                pressure = jnp.broadcast_to(pressure[:, 0:1], (8, NZ))
                for part_of in range(8):
                    term = pressure * weights[cells, pl.ds(NZ * part_of, NZ)]
                    sums[part_of] = term if part == 0 else sums[part_of] + term
            for part_of in range(8):
                buffer[2 * member + place, pl.ds(part_of, 1), :] = jnp.sum(
                    sums[part_of], axis=0, keepdims=True
                )
            return carry

        lax.fori_loop(0, 2, tile, 0)
        own = buffer.at[pl.ds(2 * member, 2)]

        def send(shift, carry):
            route(own, own, step, member_device(shift)[1]).start()
            return carry

        lax.fori_loop(1, member_count, send, 0)

    def second_leg(step):
        buffer = first[step]
        wait_bytes(buffer.at[pl.ds(0, 2 * (member_count - 1))], route_recv_sem.at[step])
        for place in range(group_count):
            second_send[step, place] = (
                buffer[index_scalars[0, place, 0]] + buffer[index_scalars[1, place, 0]]
            )
        second_recv[step, group] = second_send[step, group]

        def send(shift, carry):
            other, device = group_device(shift)
            route(
                second_send.at[step, other],
                second_recv.at[step, group],
                STEPS + step,
                device,
            ).start()
            return carry

        lax.fori_loop(1, group_count, send, 0)

    def collect(step):
        wait_bytes(
            second_recv.at[step, pl.ds(0, group_count - 1)], route_recv_sem.at[STEPS + step]
        )
        total = second_recv[step, 0]
        for place in range(1, group_count):
            total = total + second_recv[step, place]
        for part in range(8):
            loads[pl.ds(step, 1), pl.ds(NZ * part, NZ)] = total[part : part + 1, :]

    for step in range(STEPS):
        first[step][2 * member_count] = jnp.zeros((8, NZ), F32)

    for step in range(STEPS):
        interior(step)
        if step == 0:
            widen_weights()
            unpack_phases()
            find_tiles()
        if step >= 2:
            second_leg(step - 2)
        unpack(step)
        y_border(step)
        if step < STEPS - 1:
            for copy in halo_copies[step + 1][:6]:
                copy.start()
        x_border(step)
        if step < STEPS - 1:
            for copy in halo_copies[step + 1][6:]:
                copy.start()
        first_leg(step)

    results = [
        pltpu.make_async_copy(resident.at[STEPS], pops_out, local_sem.at[5]),
        pltpu.make_async_copy(mass.at[STEPS - 1], mass_out, local_sem.at[6]),
    ]
    for copy in results:
        copy.start()
    second_leg(STEPS - 2)
    for step in range(STEPS - 2):
        collect(step)
    second_leg(STEPS - 1)
    collect(STEPS - 2)
    collect(STEPS - 1)
    result = pltpu.make_async_copy(loads, loads_out, local_sem.at[7])
    result.start()
    for copy in phase_copies:
        copy.wait_send()
    for copies in halo_copies:
        for copy in copies:
            copy.wait_send()
    wait_bytes(tile_recv.at[pl.ds(0, member_count - 1)], route_send_sem.at[2 * STEPS])
    for step in range(STEPS):
        wait_bytes(first[step].at[pl.ds(0, 2 * (member_count - 1))], route_send_sem.at[step])
        wait_bytes(
            second_send.at[step, pl.ds(0, group_count - 1)], route_send_sem.at[STEPS + step]
        )
    for copy in results:
        copy.wait()
    result.wait()


def per_device(gx_count, gy_count, populations, cell_flags, fill_level, tile_block, deck_weights):
    members, groups = 2 * gy_count, gx_count // 2
    whole = pl.BlockSpec(memory_space=pl.ANY)
    pops, mass, loads = pl.pallas_call(
        functools.partial(kernel, gx_count, gy_count),
        out_shape=(
            jax.ShapeDtypeStruct((19, CELLS, NZ), F32),
            jax.ShapeDtypeStruct((CELLS, NZ), F32),
            jax.ShapeDtypeStruct((STEPS, 1024), F32),
        ),
        in_specs=[whole, whole, whole, pl.BlockSpec(memory_space=pltpu.SMEM), whole],
        out_specs=(whole, whole, whole),
        scratch_shapes=[
            pltpu.VMEM((STEPS, 18, ROWS, NZ), F32),
            pltpu.VMEM((STEPS + 1, 19, CELLS, NZ), F32),
            pltpu.VMEM((STEPS, 3, ROWS, NZ), F32),
            pltpu.VMEM((STEPS, 3, CELLS, NZ), F32),
            pltpu.VMEM((STEPS, CELLS, NZ), F32),
            pltpu.VMEM((STEPS, CELLS, NZ), F32),
            pltpu.VMEM((STEPS, CELLS, NZ), jnp.int32),
            pltpu.VMEM((CELLS, NZ), F32),
            pltpu.VMEM((CELLS, 1024), jnp.bfloat16),
            pltpu.VMEM((CELLS, 1024), F32),
            pltpu.VMEM((STEPS, 2, 5, 8, NZ), F32),
            pltpu.VMEM((STEPS, 2, 5, 8, NZ), F32),
            pltpu.VMEM((STEPS, 4, 8, NZ), F32),
            pltpu.VMEM((2, STEPS, 8, NZ), F32),
            pltpu.VMEM((2, STEPS, 8, NZ), F32),
            pltpu.VMEM((4, STEPS, 8, NZ), F32),
            pltpu.VMEM((8, NZ), jnp.int32),
            pltpu.VMEM((members, 8, NZ), jnp.int32),
            pltpu.VMEM((2, 16, NZ), jnp.int32),
            pltpu.SMEM((2, 16, NZ), jnp.int32),
            pltpu.VMEM((2 * members + 1, 8, NZ), F32),
            pltpu.VMEM((2 * members + 1, 8, NZ), F32),
            pltpu.VMEM((2 * members + 1, 8, NZ), F32),
            pltpu.VMEM((2 * members + 1, 8, NZ), F32),
            pltpu.VMEM((STEPS, groups, 8, NZ), F32),
            pltpu.VMEM((STEPS, groups, 8, NZ), F32),
            pltpu.VMEM((STEPS, 1024), F32),
            pltpu.SemaphoreType.DMA((8,)),
            pltpu.SemaphoreType.DMA((STEPS + 1, 8)),
            pltpu.SemaphoreType.DMA((STEPS + 1, 8)),
            pltpu.SemaphoreType.DMA((2 * STEPS + 1,)),
            pltpu.SemaphoreType.DMA((2 * STEPS + 1,)),
        ],
        compiler_params=pltpu.CompilerParams(
            collective_id=0, has_side_effects=True, vmem_limit_bytes=40 * 1024 * 1024
        ),
    )(
        populations.reshape(19, CELLS, NZ),
        cell_flags.reshape(STEPS, CELLS, NZ),
        fill_level.reshape(CELLS, NZ),
        tile_block,
        deck_weights.reshape(CELLS, 1024),
    )
    return (
        pops.reshape(19, CX, CY, NZ),
        mass.reshape(CX, CY, NZ),
        loads.reshape(1, STEPS, 1024),
    )


def solution(mesh):
    placed = (
        P(None, "gx", "gy", None),
        P(None, "gx", "gy", None),
        P("gx", "gy", None),
        P("gx", "gy"),
        P("gx", "gy", None, None),
    )
    return jax.shard_map(
        functools.partial(per_device, mesh.shape["gx"], mesh.shape["gy"]),
        mesh=mesh,
        in_specs=placed,
        out_specs=(P(None, "gx", "gy", None), P("gx", "gy", None), P(("gx", "gy"), None, None)),
        check_vma=False,
    )
```

```python
import functools

import jax
import jax.numpy as jnp
from jax import lax
from jax.experimental import pallas as pl
from jax.experimental.pallas import tpu as pltpu
from jax.sharding import PartitionSpec as P

velocity_table = (
    (0, 0, 0),
    (1, 0, 0),
    (-1, 0, 0),
    (0, 1, 0),
    (0, -1, 0),
    (0, 0, 1),
    (0, 0, -1),
    (1, 1, 0),
    (-1, -1, 0),
    (1, -1, 0),
    (-1, 1, 0),
    (1, 0, 1),
    (-1, 0, -1),
    (1, 0, -1),
    (-1, 0, 1),
    (0, 1, 1),
    (0, -1, -1),
    (0, 1, -1),
    (0, -1, 1),
)
weight_table = (1.0 / 3.0,) + (1.0 / 18.0,) * 6 + (1.0 / 36.0,) * 12
relax_time = 0.8
gravity = 0.001

MESH = pl.DeviceIdType.MESH
F32 = jnp.float32
STEPS = 4
CX, CY, NZ = 8, 16, 128
CELLS = CX * CY
PITCH = 24
ROWS = 248
LOW_SLAB = 8
HIGH_SLAB = PITCH * (CX + 1) + 8
X_PLUS = (1, 7, 9, 11, 13)
X_MINUS = (2, 8, 10, 12, 14)
Y_PLUS = (3, 7, 10, 15, 17)
Y_MINUS = (4, 8, 9, 16, 18)
SLOTS = X_PLUS + X_MINUS + (3, 4, 5, 6, 15, 16, 17, 18)
SLOT = {component: place for place, component in enumerate(SLOTS)}
DEEP, WIDE = 8, 4
SLAB_ROWS = CY + 2 * WIDE
FIELDS = 24
FLUID, GAS, WALL = 1.0, -0.5, -1.0


def row_of(x, y):
    return PITCH * (x + 1) + 8 + y


def turned(block, shift):
    if shift == 0:
        return block
    return pltpu.roll(block, shift % NZ, block.ndim - 1)


def version_of(shift_z):
    return 0 if shift_z == 0 else (1 if shift_z == 1 else 2)


def dot3(direction, vector):
    result = None
    for factor, part in zip(direction, vector):
        if factor == 0:
            continue
        if result is None:
            result = part if factor > 0 else -part
        else:
            result = result + part if factor > 0 else result - part
    return result


def add_momentum(totals, direction, difference):
    for axis, factor in enumerate(direction):
        if factor == 0:
            continue
        if totals[axis] is None:
            totals[axis] = difference if factor > 0 else -difference
        elif factor > 0:
            totals[axis] = totals[axis] + difference
        else:
            totals[axis] = totals[axis] - difference


def gather(own, flow, resident, pulled_of, near_of, with_mass):
    flow_square = flow[0] * flow[0] + flow[1] * flow[1] + flow[2] * flow[2]
    rest = 1.0 - 1.5 * flow_square
    rest_of = {1.0 / 18.0: rest * (2.0 / 18.0), 1.0 / 36.0: rest * (2.0 / 36.0)}
    density = resident(0)
    read = [density]
    totals = [None, None, None]
    exchanged = None
    for component in range(1, 19, 2):
        direction = velocity_table[component]
        weight = weight_table[component]
        projection = dot3(direction, flow)
        both = rest_of[weight] + (9.0 * weight) * (projection * projection)
        along = resident(component)
        against = resident(component + 1)
        for place, reverse in ((component, against), (component + 1, along)):
            pulled = pulled_of(place)
            near = near_of(place)
            read.append(
                jnp.where(near < -0.25, jnp.where(near < -0.75, reverse, both - reverse), pulled)
            )
            if with_mass:
                share = jnp.minimum(jnp.maximum(own + near, 0.0), 1.0)
                moved = share * (pulled - reverse)
                exchanged = moved if exchanged is None else exchanged + moved
        density = density + (read[component] + read[component + 1])
        add_momentum(totals, direction, read[component] - read[component + 1])
    return read, density, totals, exchanged


def relax(read, density, totals, put):
    speed = [totals[0], totals[1], totals[2] - relax_time * gravity]
    speed_square = speed[0] * speed[0] + speed[1] * speed[1] + speed[2] * speed[2]
    base = density - 1.5 * speed_square
    gain = 1.0 / relax_time
    keep = 1.0 - gain
    put(0, (gain * weight_table[0]) * base + keep * read[0])
    base_of = {1.0 / 18.0: base * (gain / 18.0), 1.0 / 36.0: base * (gain / 36.0)}
    for component in range(1, 19, 2):
        weight = weight_table[component]
        projection = dot3(velocity_table[component], speed)
        even = base_of[weight] + (4.5 * gain * weight) * (projection * projection)
        odd = (3.0 * gain * weight) * projection
        put(component, (even + odd) + keep * read[component])
        put(component + 1, (even - odd) + keep * read[component + 1])


def momentum_after(totals):
    return [totals[0], totals[1], totals[2] - gravity]


def rolled(block, shift):
    shift = shift % NZ
    return block if shift == 0 else pltpu.roll(block, shift, block.ndim - 1)


def slab_shift(direction):
    return DEEP * direction[0] + direction[2]


def slab_version(direction):
    return 3 * (direction[0] + 1) + direction[2] + 1


def kernel(
    gx_count,
    gy_count,
    pops_in,
    flags_in,
    fill_in,
    tile_in,
    weights_in,
    pops_out,
    mass_out,
    loads_out,
    streamed,
    resident,
    phases,
    current,
    mass,
    flags,
    fill,
    weights_packed,
    weights,
    y_send,
    y_recv,
    corner_recv,
    hy_send,
    hy_recv,
    hcorner_recv,
    tile_send,
    tile_recv,
    index_block,
    index_scalars,
    slab,
    slab_resident,
    slab_streamed,
    slab_phases,
    slab_current,
    slab_deck,
    x_pack,
    y_pack,
    corner_pack,
    x_pack_recv,
    y_pack_recv,
    corner_pack_recv,
    tile_scalars,
    first,
    second_send,
    second_recv,
    loads,
    local_sem,
    halo_send_sem,
    halo_recv_sem,
    route_send_sem,
    route_recv_sem,
):
    gx = lax.axis_index("gx")
    gy = lax.axis_index("gy")
    group_count = gx_count // 2
    member_count = 2 * gy_count
    group = gx // 2
    member = lax.rem(gx, 2) * gy_count + gy
    east = lax.rem(gx + 1, gx_count)
    west = lax.rem(gx + gx_count - 1, gx_count)
    north = lax.rem(gy + 1, gy_count)
    south = lax.rem(gy + gy_count - 1, gy_count)

    def member_device(shift):
        other = lax.rem(member + shift, member_count)
        return other, (2 * group + other // gy_count, lax.rem(other, gy_count))

    def group_device(shift):
        other = lax.rem(group + shift, group_count)
        return other, (2 * other + lax.rem(gx, 2), gy)

    neighbours = (
        (east, gy),
        (west, gy),
        (gx, north),
        (gx, south),
        (east, north),
        (west, south),
        (east, south),
        (west, north),
    )

    loads_of = [
        pltpu.make_async_copy(flags_in, flags, local_sem.at[0]),
        pltpu.make_async_copy(fill_in, fill, local_sem.at[1]),
        pltpu.make_async_copy(pops_in, resident.at[0], local_sem.at[2]),
        pltpu.make_async_copy(weights_in, weights_packed, local_sem.at[3]),
        pltpu.make_async_copy(tile_in, tile_scalars, local_sem.at[8]),
    ]
    for copy in loads_of:
        copy.start()

    barrier = pltpu.get_barrier_semaphore()
    for device in neighbours:
        pl.semaphore_signal(barrier, inc=1, device_id=device, device_id_type=MESH)
    for shift in range(1, member_count):
        pl.semaphore_signal(
            barrier, inc=1, device_id=member_device(shift)[1], device_id_type=MESH
        )
    for shift in range(1, group_count):
        pl.semaphore_signal(
            barrier, inc=1, device_id=group_device(shift)[1], device_id_type=MESH
        )

    lane = lax.broadcasted_iota(jnp.int32, (8, NZ), 1)

    def put_phase(step, rows, code):
        phases[step, 0, rows, :] = code
        phases[step, 1, rows, :] = jnp.where(lane == 0, WALL, turned(code, 1))
        phases[step, 2, rows, :] = jnp.where(lane == NZ - 1, GAS, turned(code, -1))

    loads_of[0].wait()
    loads_of[1].wait()

    def code_rows(index, carry):
        x = index // 2
        half = lax.rem(index, 2)
        cells = pl.ds(pl.multiple_of(8 * index, 8), 8)
        rows = pl.ds(pl.multiple_of(PITCH * x + 32 + 8 * half, 8), 8)
        level = 0.5 * fill[cells, :]
        for step in range(STEPS):
            kind = flags[step, cells, :]
            code = jnp.where(
                kind == 0, FLUID, jnp.where(kind == 1, level, jnp.where(kind == 2, GAS, WALL))
            )
            put_phase(step, rows, code)
        return carry

    lax.fori_loop(0, 2 * CX, code_rows, 0)
    for step in range(STEPS):
        hy_send[0, step] = phases[step, 0, pl.ds(row_of(0, CY - 1), CX, stride=PITCH), :]
        hy_send[1, step] = phases[step, 0, pl.ds(row_of(0, 0), CX, stride=PITCH), :]

    loads_of[2].wait()

    def first_rows(index, carry):
        x = index // 2
        half = lax.rem(index, 2)
        cells = pl.ds(pl.multiple_of(8 * index, 8), 8)
        rows = pl.ds(pl.multiple_of(PITCH * x + 32 + 8 * half, 8), 8)
        totals = [None, None, None]
        for component in range(1, 19, 2):
            direction = velocity_table[component]
            along = resident[0, component, cells, :]
            against = resident[0, component + 1, cells, :]
            add_momentum(totals, direction, along - against)
            streamed[0, SLOT[component], rows, :] = turned(along, direction[2])
            streamed[0, SLOT[component + 1], rows, :] = turned(against, -direction[2])
        for axis in range(3):
            current[0, axis, cells, :] = totals[axis]
        return carry

    lax.fori_loop(0, 2 * CX, first_rows, 0)
    for side, (y, components) in enumerate(((CY - 1, Y_PLUS), (0, Y_MINUS))):
        for place, component in enumerate(components):
            y_send[0, side, place] = turned(
                resident[0, component, pl.ds(y, CX, stride=CY), :], velocity_table[component][2]
            )

    pl.semaphore_wait(barrier, 8 + member_count - 1 + group_count - 1)

    def remote(source, target, exchange, place, device):
        return pltpu.make_async_remote_copy(
            src_ref=source,
            dst_ref=target,
            send_sem=halo_send_sem.at[exchange, place],
            recv_sem=halo_recv_sem.at[exchange, place],
            device_id=device,
            device_id_type=MESH,
        )

    def y_copies(step):
        return [
            remote(y_send.at[step, 0, 1], corner_recv.at[step, 0], step, 4, neighbours[4]),
            remote(y_send.at[step, 1, 1], corner_recv.at[step, 1], step, 5, neighbours[5]),
            remote(y_send.at[step, 1, 2], corner_recv.at[step, 2], step, 6, neighbours[6]),
            remote(y_send.at[step, 0, 2], corner_recv.at[step, 3], step, 7, neighbours[7]),
            remote(y_send.at[step, 0], y_recv.at[step, 0], step, 2, neighbours[2]),
            remote(y_send.at[step, 1], y_recv.at[step, 1], step, 3, neighbours[3]),
        ]

    def x_copies(step):
        return [
            remote(
                streamed.at[step, pl.ds(0, 5), pl.ds(row_of(CX - 1, 0), CY), :],
                streamed.at[step, pl.ds(0, 5), pl.ds(LOW_SLAB, CY), :],
                step,
                0,
                neighbours[0],
            ),
            remote(
                streamed.at[step, pl.ds(5, 5), pl.ds(row_of(0, 0), CY), :],
                streamed.at[step, pl.ds(5, 5), pl.ds(HIGH_SLAB, CY), :],
                step,
                1,
                neighbours[1],
            ),
        ]

    phase_copies = [
        remote(
            phases.at[:, 0, pl.ds(row_of(CX - 1, 0), CY), :],
            phases.at[:, 0, pl.ds(LOW_SLAB, CY), :],
            STEPS,
            0,
            neighbours[0],
        ),
        remote(
            phases.at[:, 0, pl.ds(row_of(0, 0), CY), :],
            phases.at[:, 0, pl.ds(HIGH_SLAB, CY), :],
            STEPS,
            1,
            neighbours[1],
        ),
        remote(hy_send.at[0], hy_recv.at[0], STEPS, 2, neighbours[2]),
        remote(hy_send.at[1], hy_recv.at[1], STEPS, 3, neighbours[3]),
        remote(hy_send.at[0], hcorner_recv.at[0], STEPS, 4, neighbours[4]),
        remote(hy_send.at[1], hcorner_recv.at[1], STEPS, 5, neighbours[5]),
        remote(hy_send.at[1], hcorner_recv.at[2], STEPS, 6, neighbours[6]),
        remote(hy_send.at[0], hcorner_recv.at[3], STEPS, 7, neighbours[7]),
    ]
    halo_copies = [y_copies(step) + x_copies(step) for step in range(STEPS)]
    slab_copies = [
        remote(x_pack.at[0], x_pack_recv.at[0], STEPS + 1, 0, neighbours[0]),
        remote(x_pack.at[1], x_pack_recv.at[1], STEPS + 1, 1, neighbours[1]),
        remote(y_pack.at[0], y_pack_recv.at[0], STEPS + 1, 2, neighbours[2]),
        remote(y_pack.at[1], y_pack_recv.at[1], STEPS + 1, 3, neighbours[3]),
        remote(corner_pack.at[0], corner_pack_recv.at[0], STEPS + 1, 4, neighbours[4]),
        remote(corner_pack.at[1], corner_pack_recv.at[1], STEPS + 1, 5, neighbours[5]),
        remote(corner_pack.at[2], corner_pack_recv.at[2], STEPS + 1, 6, neighbours[6]),
        remote(corner_pack.at[3], corner_pack_recv.at[3], STEPS + 1, 7, neighbours[7]),
    ]
    for copy in halo_copies[0]:
        copy.start()
    for copy in phase_copies:
        copy.start()

    lane4 = lax.broadcasted_iota(jnp.int32, (4, NZ), 1)

    def into_slab(block_of):
        gathered = None
        for x in range(CX):
            block = rolled(block_of(x), DEEP * (x + WIDE))
            gathered = block if x == 0 else jnp.where(lane >= DEEP * (x + WIDE), block, gathered)
        return gathered

    def slab_population(component, carry):
        for half in (0, 8):
            slab[component, pl.ds(WIDE + half, 8), :] = into_slab(
                lambda x: resident[0, component, pl.ds(CY * x + half, 8), :]
            )
        return carry

    def slab_phase(step, carry):
        for half in (0, 8):
            slab[19 + step, pl.ds(WIDE + half, 8), :] = into_slab(
                lambda x: phases[step, 0, pl.ds(row_of(x, half), 8), :]
            )
        return carry

    lax.fori_loop(0, 19, slab_population, 0)
    lax.fori_loop(0, STEPS, slab_phase, 0)
    slab[FIELDS - 1] = jnp.zeros((SLAB_ROWS, NZ), F32)

    def pack(part, carry):
        for half in (0, 1):
            blocks = [slab[4 * part + j, pl.ds(WIDE + 8 * half, 8), :] for j in range(4)]
            for side, start in ((0, 64), (1, 32)):
                packed = rolled(blocks[0], -start)
                for j in (1, 2, 3):
                    packed = jnp.where(lane >= 32 * j, rolled(blocks[j], 32 * j - start), packed)
                x_pack[side, part, pl.ds(8 * half, 8), :] = packed
            for j in (0, 1):
                packed = jnp.where(
                    lane < 64, rolled(blocks[2 * j], -32), rolled(blocks[2 * j + 1], 32)
                )
                if half == 1:
                    y_pack[0, part, pl.ds(4 * j, 4), :] = packed[4:8, :]
                else:
                    y_pack[1, part, pl.ds(4 * j, 4), :] = packed[0:4, :]
        return carry

    lax.fori_loop(0, FIELDS // 4, pack, 0)
    for part in range(FIELDS // 4):
        rows = pl.ds(4 * (part % 2), 4)
        corner_pack[0, part // 2, rows, :] = x_pack[0, part, pl.ds(12, 4), :]
        corner_pack[1, part // 2, rows, :] = x_pack[1, part, pl.ds(0, 4), :]
        corner_pack[2, part // 2, rows, :] = x_pack[0, part, pl.ds(0, 4), :]
        corner_pack[3, part // 2, rows, :] = x_pack[1, part, pl.ds(12, 4), :]
    for copy in slab_copies:
        copy.start()

    loads_of[4].wait()
    tile_send[...] = jnp.where(
        lane == 2 * member,
        tile_scalars[0, 0],
        jnp.where(lane == 2 * member + 1, tile_scalars[0, 1], 0),
    )
    tile_recv[member] = tile_send[...]

    def route(source, target, kind, device):
        return pltpu.make_async_remote_copy(
            src_ref=source,
            dst_ref=target,
            send_sem=route_send_sem.at[kind],
            recv_sem=route_recv_sem.at[kind],
            device_id=device,
            device_id_type=MESH,
        )

    def wait_bytes(ref, semaphore):
        pltpu.make_async_copy(ref, ref, semaphore).wait()

    def tell_members(shift, carry):
        route(tile_send, tile_recv.at[member], 0, member_device(shift)[1]).start()
        return carry

    lax.fori_loop(1, member_count, tell_members, 0)

    def update(step, prow, crow, column=None):
        final = step == STEPS - 1
        pstep, cstep = (PITCH, CY) if column is not None else (None, None)

        def rows(offset):
            if pstep is None:
                return pl.ds(prow + offset, 8)
            return pl.ds(prow + offset, 8, stride=pstep)

        cells = pl.ds(crow, 8) if cstep is None else pl.ds(crow, 8, stride=cstep)
        own = phases[step, 0, rows(0), :]
        liquid = own > -0.25
        offsets = [PITCH * direction[0] + direction[1] for direction in velocity_table]
        read, density, totals, exchanged = gather(
            own,
            [current[step, axis, cells, :] for axis in range(3)],
            lambda component: resident[step, component, cells, :],
            lambda component: streamed[step, SLOT[component], rows(-offsets[component]), :],
            lambda component: phases[
                step, version_of(velocity_table[component][2]), rows(-offsets[component]), :
            ],
            True,
        )
        interface = jnp.logical_and(liquid, own < 0.75)
        exchanged = jnp.where(interface, exchanged, 0.0)
        if step > 0:
            exchanged = exchanged + mass[step - 1, cells, :]
        mass[step, cells, :] = exchanged

        def put(component, value):
            value = jnp.where(liquid, value, weight_table[component])
            resident[step + 1, component, cells, :] = value
            if final or component == 0:
                return
            value = turned(value, velocity_table[component][2])
            streamed[step + 1, SLOT[component], rows(0), :] = value
            if column is not None:
                side, names = (0, Y_PLUS) if column > 0 else (1, Y_MINUS)
                if component in names:
                    y_send[step + 1, side, names.index(component)] = value

        relax(read, density, totals, put)
        if not final:
            for axis, value in enumerate(momentum_after(totals)):
                current[step + 1, axis, cells, :] = jnp.where(liquid, value, 0.0)

    def interior(step):
        def slab(x, carry):
            for y in (1, 7):
                update(step, PITCH * x + PITCH + 8 + y, CY * x + y)
            return carry

        lax.fori_loop(1, CX - 1, slab, 0)

    def y_border(step):
        for y in (0, CY - 1):
            update(step, row_of(0, y), y, column=y)

    def x_border(step):
        def slab(index, carry):
            x = (CX - 1) * (index // 2)
            half = 8 * lax.rem(index, 2)
            update(
                step,
                pl.multiple_of(PITCH * x + PITCH + 8 + half, 8),
                pl.multiple_of(CY * x + half, 8),
            )
            return carry

        lax.fori_loop(0, 4, slab, 0)

    corners = (
        (7, row_of(-1, -1), CX - 1),
        (8, row_of(CX, CY), 0),
        (9, row_of(-1, CY), CX - 1),
        (10, row_of(CX, -1), 0),
    )

    def unpack(step):
        for copy in halo_copies[step]:
            copy.wait_recv()
        for side, (y, names) in enumerate(((-1, Y_PLUS), (CY, Y_MINUS))):
            for place, component in enumerate(names):
                streamed[step, SLOT[component], pl.ds(row_of(0, y), CX, stride=PITCH), :] = y_recv[
                    step, side, place
                ]
        for place, (component, row, x) in enumerate(corners):
            streamed[step, SLOT[component], pl.ds(row, 1), :] = corner_recv[
                step, place, pl.ds(x, 1), :
            ]

    def unpack_phases():
        for copy in phase_copies:
            copy.wait_recv()
        at_west, at_east = gx == 0, gx == gx_count - 1
        at_south, at_north = gy == 0, gy == gy_count - 1

        def one(step, carry):
            for start, edge in ((LOW_SLAB, at_west), (HIGH_SLAB, at_east)):
                for half in (0, 8):
                    rows = pl.ds(start + half, 8)
                    put_phase(step, rows, jnp.where(edge, GAS, phases[step, 0, rows, :]))
            for side, (y, edge) in enumerate(((-1, at_south), (CY, at_north))):
                rows = pl.ds(row_of(0, y), CX, stride=PITCH)
                put_phase(step, rows, jnp.where(edge, GAS, hy_recv[side, step]))
            edges = (
                at_west | at_south,
                at_east | at_north,
                at_west | at_north,
                at_east | at_south,
            )
            for place, (component, row, x) in enumerate(corners):
                code = hcorner_recv[place, step, pl.ds(x, 1), :]
                phases[step, 0, pl.ds(row, 1), :] = jnp.where(edges[place], GAS, code)
            return carry

        lax.fori_loop(0, STEPS, one, 0)

    def find_tiles():
        wait_bytes(tile_recv.at[pl.ds(0, member_count - 1)], route_recv_sem.at[0])
        names = tile_recv[0]
        for place in range(1, member_count):
            names = names + tile_recv[place]
        sublane = lax.broadcasted_iota(jnp.int32, (8, NZ), 0)
        none = 2 * member_count
        for part in range((group_count + 7) // 8):
            wanted = (sublane + 8 * part) * member_count + member
            match = jnp.logical_and(names == wanted, lane < none)
            last = jnp.max(jnp.where(match, lane, -1), axis=1, keepdims=True)
            early = jnp.min(jnp.where(match, lane, none), axis=1, keepdims=True)
            early = jnp.where(early == last, none, early)
            last = jnp.where(last < 0, none, last)
            index_block[0, pl.ds(8 * part, 8), :] = jnp.broadcast_to(last, (8, NZ))
            index_block[1, pl.ds(8 * part, 8), :] = jnp.broadcast_to(early, (8, NZ))
        copy = pltpu.make_async_copy(index_block, index_scalars, local_sem.at[4])
        copy.start()
        copy.wait()

    def widen_weights():
        loads_of[3].wait()
        for part in range(CELLS // 16):
            rows = pl.ds(16 * part, 16)
            weights[rows, :] = weights_packed[rows, :].astype(F32)

    def unpack_slab():
        for copy in slab_copies:
            copy.wait_recv()

        def fields(part, carry):
            quarter = pl.ds(4 * lax.rem(part, 2), 4)
            for j in range(4):
                field = 4 * part + j
                for half in (0, 8):
                    rows = pl.ds(WIDE + half, 8)
                    low = rolled(x_pack_recv[0, part, pl.ds(half, 8), :], -32 * j)
                    high = rolled(x_pack_recv[1, part, pl.ds(half, 8), :], 96 - 32 * j)
                    slab[field, rows, :] = jnp.where(
                        lane < 32, low, jnp.where(lane >= 96, high, slab[field, rows, :])
                    )
                for side, row, west_corner, east_corner in ((0, 0, 0, 3), (1, CY + WIDE, 2, 1)):
                    middle = rolled(
                        y_pack_recv[side, part, pl.ds(4 * (j // 2), 4), :], 32 - 64 * (j % 2)
                    )
                    low = rolled(corner_pack_recv[west_corner, part // 2, quarter, :], -32 * j)
                    high = rolled(corner_pack_recv[east_corner, part // 2, quarter, :], 96 - 32 * j)
                    slab[field, pl.ds(row, 4), :] = jnp.where(
                        lane4 < 32, low, jnp.where(lane4 >= 96, high, middle)
                    )
            return carry

        lax.fori_loop(0, FIELDS // 4, fields, 0)
        low_lane = jnp.where(gx == 0, DEEP * WIDE, 0)
        high_lane = jnp.where(gx == gx_count - 1, NZ - DEEP * WIDE, NZ)
        low_row = jnp.where(gy == 0, WIDE, 0)
        high_row = jnp.where(gy == gy_count - 1, CY + WIDE, SLAB_ROWS)
        level = lax.rem(lane, DEEP)

        def ready(block, carry):
            start = pl.multiple_of(8 * block, 8)
            cells = pl.ds(start, 8)
            rows = pl.ds(pl.multiple_of(start + 8, 8), 8)
            totals = [None, None, None]
            for component in range(1, 19, 2):
                direction = velocity_table[component]
                along = slab[component, cells, :]
                against = slab[component + 1, cells, :]
                add_momentum(totals, direction, along - against)
                shift = slab_shift(direction)
                slab_streamed[0, SLOT[component], rows, :] = rolled(along, shift)
                slab_streamed[0, SLOT[component + 1], rows, :] = rolled(against, -shift)
            for axis in range(3):
                slab_current[0, axis, cells, :] = totals[axis]
            row = lax.broadcasted_iota(jnp.int32, (8, NZ), 0) + start
            inside = jnp.logical_and(
                jnp.logical_and(lane >= low_lane, lane < high_lane),
                jnp.logical_and(row >= low_row, row < high_row),
            )
            for step in range(STEPS):
                code = jnp.where(inside, slab[19 + step, cells, :], GAS)
                for shift_x in (-1, 0, 1):
                    for shift_z in (-1, 0, 1):
                        direction = (shift_x, 0, shift_z)
                        value = rolled(code, slab_shift(direction))
                        if shift_z == 1:
                            value = jnp.where(level == 0, WALL, value)
                        slab_phases[step, slab_version(direction), rows, :] = value
            return carry

        lax.fori_loop(0, SLAB_ROWS // 8, ready, 0)

    def slab_update(step, start):
        cells = pl.ds(start, 8)

        def rows(offset):
            return pl.ds(start + 8 + offset, 8)

        def own_of(component):
            if step == 0:
                return slab[component, cells, :]
            return slab_resident[step - 1, component, cells, :]

        own = slab_phases[step, slab_version((0, 0, 0)), rows(0), :]
        liquid = own > -0.25
        read, density, totals, _ = gather(
            own,
            [slab_current[step, axis, cells, :] for axis in range(3)],
            own_of,
            lambda component: slab_streamed[
                step, SLOT[component], rows(-velocity_table[component][1]), :
            ],
            lambda component: slab_phases[
                step,
                slab_version(velocity_table[component]),
                rows(-velocity_table[component][1]),
                :,
            ],
            False,
        )
        slab_deck[step, cells, :] = jnp.where(liquid, density * (1.0 / 3.0), 0.0)
        if step == STEPS - 1:
            return

        def put(component, value):
            value = jnp.where(liquid, value, weight_table[component])
            slab_resident[step, component, cells, :] = value
            if component > 0:
                slab_streamed[step + 1, SLOT[component], rows(0), :] = rolled(
                    value, slab_shift(velocity_table[component])
                )

        relax(read, density, totals, put)
        for axis, value in enumerate(momentum_after(totals)):
            slab_current[step + 1, axis, cells, :] = jnp.where(liquid, value, 0.0)

    def slab_steps():
        for step in range(STEPS - 1):

            def block(index, carry, step=step):
                slab_update(step, pl.multiple_of(8 * index, 8))
                return carry

            lax.fori_loop(0, SLAB_ROWS // 8, block, 0)
        for start in (WIDE, WIDE + 8):
            slab_update(STEPS - 1, start)

    def first_leg():
        def one(step, carry):
            for tile in range(2):
                sums = [None] * 8
                for part in range(8):
                    x = 4 * tile + part // 2
                    cells = pl.ds(64 * tile + 8 * part, 8)
                    pressure = slab_deck[step, pl.ds(WIDE + 8 * (part % 2), 8), :]
                    pressure = pressure.astype(jnp.bfloat16).astype(F32)
                    place = DEEP * (x + WIDE)
                    pressure = jnp.broadcast_to(pressure[:, place : place + 1], (8, NZ))
                    for column in range(8):
                        term = pressure * weights[cells, pl.ds(NZ * column, NZ)]
                        sums[column] = term if part == 0 else sums[column] + term
                for column in range(8):
                    first[2 * member + tile, step, pl.ds(column, 1), :] = jnp.sum(
                        sums[column], axis=0, keepdims=True
                    )
            return carry

        lax.fori_loop(0, STEPS, one, 0)
        own = first.at[pl.ds(2 * member, 2)]

        def send(shift, carry):
            route(own, own, 1, member_device(shift)[1]).start()
            return carry

        lax.fori_loop(1, member_count, send, 0)

    def second_leg():
        wait_bytes(first.at[pl.ds(0, 2 * (member_count - 1))], route_recv_sem.at[1])
        for place in range(group_count):
            second_send[place] = first[index_scalars[0, place, 0]] + first[index_scalars[1, place, 0]]
        second_recv[group] = second_send[group]

        def send(shift, carry):
            other, device = group_device(shift)
            route(second_send.at[other], second_recv.at[group], 2, device).start()
            return carry

        lax.fori_loop(1, group_count, send, 0)

    def collect():
        wait_bytes(second_recv.at[pl.ds(0, group_count - 1)], route_recv_sem.at[2])
        for step in range(STEPS):
            total = second_recv[0, step]
            for place in range(1, group_count):
                total = total + second_recv[place, step]
            for column in range(8):
                loads[pl.ds(step, 1), pl.ds(NZ * column, NZ)] = total[column : column + 1, :]

    first[2 * member_count] = jnp.zeros((STEPS, 8, NZ), F32)

    for step in range(STEPS):
        interior(step)
        if step == 0:
            widen_weights()
            unpack_phases()
            find_tiles()
        if step == 1:
            unpack_slab()
            slab_steps()
            first_leg()
        if step == 2:
            second_leg()
        unpack(step)
        y_border(step)
        if step < STEPS - 1:
            for copy in halo_copies[step + 1][:6]:
                copy.start()
        x_border(step)
        if step < STEPS - 1:
            for copy in halo_copies[step + 1][6:]:
                copy.start()

    results = [
        pltpu.make_async_copy(resident.at[STEPS], pops_out, local_sem.at[5]),
        pltpu.make_async_copy(mass.at[STEPS - 1], mass_out, local_sem.at[6]),
    ]
    for copy in results:
        copy.start()
    collect()
    result = pltpu.make_async_copy(loads, loads_out, local_sem.at[7])
    result.start()
    for copy in phase_copies:
        copy.wait_send()
    for copy in slab_copies:
        copy.wait_send()
    for copies in halo_copies:
        for copy in copies:
            copy.wait_send()
    wait_bytes(tile_recv.at[pl.ds(0, member_count - 1)], route_send_sem.at[0])
    wait_bytes(first.at[pl.ds(0, 2 * (member_count - 1))], route_send_sem.at[1])
    wait_bytes(second_send.at[pl.ds(0, group_count - 1)], route_send_sem.at[2])
    for copy in results:
        copy.wait()
    result.wait()


def hand_over(pops, mass, loads, pops_out, mass_out, loads_out, semaphores):
    copies = [
        pltpu.make_async_copy(pops, pops_out, semaphores.at[0]),
        pltpu.make_async_copy(mass, mass_out, semaphores.at[1]),
        pltpu.make_async_copy(loads, loads_out, semaphores.at[2]),
    ]
    for copy in copies:
        copy.start()
    for copy in copies:
        copy.wait()


def per_device(gx_count, gy_count, populations, cell_flags, fill_level, tile_block, deck_weights):
    members, groups = 2 * gy_count, gx_count // 2
    whole = pl.BlockSpec(memory_space=pltpu.HBM)
    keep = pl.BlockSpec(memory_space=pl.ANY)
    placed = functools.partial(pltpu.with_memory_space_constraint, memory_space=pltpu.HBM)
    pops, mass, loads = pl.pallas_call(
        functools.partial(kernel, gx_count, gy_count),
        out_shape=(
            pltpu.VMEM((19, CELLS, NZ), F32),
            pltpu.VMEM((CELLS, NZ), F32),
            pltpu.VMEM((STEPS, 1024), F32),
        ),
        in_specs=[whole] * 5,
        out_specs=(keep, keep, keep),
        scratch_shapes=[
            pltpu.VMEM((STEPS, 18, ROWS, NZ), F32),
            pltpu.VMEM((STEPS + 1, 19, CELLS, NZ), F32),
            pltpu.VMEM((STEPS, 3, ROWS, NZ), F32),
            pltpu.VMEM((STEPS, 3, CELLS, NZ), F32),
            pltpu.VMEM((STEPS, CELLS, NZ), F32),
            pltpu.VMEM((STEPS, CELLS, NZ), jnp.int32),
            pltpu.VMEM((CELLS, NZ), F32),
            pltpu.VMEM((CELLS, 1024), jnp.bfloat16),
            pltpu.VMEM((CELLS, 1024), F32),
            pltpu.VMEM((STEPS, 2, 5, 8, NZ), F32),
            pltpu.VMEM((STEPS, 2, 5, 8, NZ), F32),
            pltpu.VMEM((STEPS, 4, 8, NZ), F32),
            pltpu.VMEM((2, STEPS, 8, NZ), F32),
            pltpu.VMEM((2, STEPS, 8, NZ), F32),
            pltpu.VMEM((4, STEPS, 8, NZ), F32),
            pltpu.VMEM((8, NZ), jnp.int32),
            pltpu.VMEM((members, 8, NZ), jnp.int32),
            pltpu.VMEM((2, 16, NZ), jnp.int32),
            pltpu.SMEM((2, 16, NZ), jnp.int32),
            pltpu.VMEM((FIELDS, SLAB_ROWS, NZ), F32),
            pltpu.VMEM((STEPS - 1, 19, SLAB_ROWS, NZ), F32),
            pltpu.VMEM((STEPS, 18, SLAB_ROWS + 16, NZ), F32),
            pltpu.VMEM((STEPS, 9, SLAB_ROWS + 16, NZ), F32),
            pltpu.VMEM((STEPS, 3, SLAB_ROWS, NZ), F32),
            pltpu.VMEM((STEPS, SLAB_ROWS, NZ), F32),
            pltpu.VMEM((2, FIELDS // 4, CY, NZ), F32),
            pltpu.VMEM((2, FIELDS // 4, 8, NZ), F32),
            pltpu.VMEM((4, FIELDS // 8, 8, NZ), F32),
            pltpu.VMEM((2, FIELDS // 4, CY, NZ), F32),
            pltpu.VMEM((2, FIELDS // 4, 8, NZ), F32),
            pltpu.VMEM((4, FIELDS // 8, 8, NZ), F32),
            pltpu.SMEM((1, 2), jnp.int32),
            pltpu.VMEM((2 * members + 1, STEPS, 8, NZ), F32),
            pltpu.VMEM((groups, STEPS, 8, NZ), F32),
            pltpu.VMEM((groups, STEPS, 8, NZ), F32),
            pltpu.VMEM((STEPS, 1024), F32),
            pltpu.SemaphoreType.DMA((9,)),
            pltpu.SemaphoreType.DMA((STEPS + 2, 8)),
            pltpu.SemaphoreType.DMA((STEPS + 2, 8)),
            pltpu.SemaphoreType.DMA((3,)),
            pltpu.SemaphoreType.DMA((3,)),
        ],
        compiler_params=pltpu.CompilerParams(
            collective_id=0, has_side_effects=True, vmem_limit_bytes=32 * 1024 * 1024
        ),
    )(
        placed(populations.reshape(19, CELLS, NZ)),
        placed(cell_flags.reshape(STEPS, CELLS, NZ)),
        placed(fill_level.reshape(CELLS, NZ)),
        placed(tile_block.reshape(1, 2)),
        placed(deck_weights.reshape(CELLS, 1024)),
    )
    pops, mass, loads = pl.pallas_call(
        hand_over,
        out_shape=(
            pltpu.HBM((19, CELLS, NZ), F32),
            pltpu.HBM((CELLS, NZ), F32),
            pltpu.HBM((STEPS, 1024), F32),
        ),
        in_specs=[keep] * 3,
        out_specs=(whole, whole, whole),
        scratch_shapes=[pltpu.SemaphoreType.DMA((3,))],
    )(*(pltpu.with_memory_space_constraint(part, pltpu.VMEM) for part in (pops, mass, loads)))
    return (
        pops.reshape(19, CX, CY, NZ),
        mass.reshape(CX, CY, NZ),
        loads.reshape(1, STEPS, 1024),
    )


def solution(mesh):
    placed = (
        P(None, "gx", "gy", None),
        P(None, "gx", "gy", None),
        P("gx", "gy", None),
        P("gx", "gy"),
        P("gx", "gy", None, None),
    )
    return jax.shard_map(
        functools.partial(per_device, mesh.shape["gx"], mesh.shape["gy"]),
        mesh=mesh,
        in_specs=placed,
        out_specs=(P(None, "gx", "gy", None), P("gx", "gy", None), P(("gx", "gy"), None, None)),
        check_vma=False,
    )
```

```python
import functools

import jax
import jax.numpy as jnp
from jax import lax
from jax.experimental import pallas as pl
from jax.experimental.pallas import tpu as pltpu
from jax.sharding import PartitionSpec as P

velocity_table = (
    (0, 0, 0),
    (1, 0, 0),
    (-1, 0, 0),
    (0, 1, 0),
    (0, -1, 0),
    (0, 0, 1),
    (0, 0, -1),
    (1, 1, 0),
    (-1, -1, 0),
    (1, -1, 0),
    (-1, 1, 0),
    (1, 0, 1),
    (-1, 0, -1),
    (1, 0, -1),
    (-1, 0, 1),
    (0, 1, 1),
    (0, -1, -1),
    (0, 1, -1),
    (0, -1, 1),
)
weight_table = (1.0 / 3.0,) + (1.0 / 18.0,) * 6 + (1.0 / 36.0,) * 12
relax_time = 0.8
gravity = 0.001

MESH = pl.DeviceIdType.MESH
F32 = jnp.float32
STEPS = 4
CX, CY, NZ = 8, 16, 128
CELLS = CX * CY
PITCH = 24
ROWS = 248
LOW_SLAB = 8
HIGH_SLAB = PITCH * (CX + 1) + 8
X_PLUS = (1, 7, 9, 11, 13)
X_MINUS = (2, 8, 10, 12, 14)
Y_PLUS = (3, 7, 10, 15, 17)
Y_MINUS = (4, 8, 9, 16, 18)
SLOTS = X_PLUS + X_MINUS + (3, 4, 5, 6, 15, 16, 17, 18)
SLOT = {component: place for place, component in enumerate(SLOTS)}
DEEP, WIDE = 8, 4
SLAB_ROWS = CY + 2 * WIDE
FIELDS = 24
FLUID, GAS, WALL = 1.0, -0.5, -1.0


def aligned(value, unit):
    return value if isinstance(value, int) else pl.multiple_of(value, unit)


def remainder(value, unit):
    return value % unit if isinstance(value, int) else lax.rem(value, unit)


def loop(low, high, body, group):
    if group >= high - low:
        for index in range(low, high):
            body(index, 0)
        return
    turns = (high - low) // group

    def turn(index, carry):
        for place in range(group):
            body(low + index * group + place, 0)
        return carry

    lax.fori_loop(0, turns, turn, 0)


def row_of(x, y):
    return PITCH * (x + 1) + 8 + y


def turned(block, shift):
    if shift == 0:
        return block
    return pltpu.roll(block, shift % NZ, block.ndim - 1)


def version_of(shift_z):
    return 0 if shift_z == 0 else (1 if shift_z == 1 else 2)


def dot3(direction, vector):
    result = None
    for factor, part in zip(direction, vector):
        if factor == 0:
            continue
        if result is None:
            result = part if factor > 0 else -part
        else:
            result = result + part if factor > 0 else result - part
    return result


def add_momentum(totals, direction, difference):
    for axis, factor in enumerate(direction):
        if factor == 0:
            continue
        if totals[axis] is None:
            totals[axis] = difference if factor > 0 else -difference
        elif factor > 0:
            totals[axis] = totals[axis] + difference
        else:
            totals[axis] = totals[axis] - difference


def gather(own, flow, resident, pulled_of, near_of, with_mass):
    flow_square = flow[0] * flow[0] + flow[1] * flow[1] + flow[2] * flow[2]
    rest = 1.0 - 1.5 * flow_square
    rest_of = {1.0 / 18.0: rest * (2.0 / 18.0), 1.0 / 36.0: rest * (2.0 / 36.0)}
    density = resident(0)
    read = [density]
    totals = [None, None, None]
    exchanged = None
    for component in range(1, 19, 2):
        direction = velocity_table[component]
        weight = weight_table[component]
        projection = dot3(direction, flow)
        both = rest_of[weight] + (9.0 * weight) * (projection * projection)
        along = resident(component)
        against = resident(component + 1)
        for place, reverse in ((component, against), (component + 1, along)):
            pulled = pulled_of(place)
            near = near_of(place)
            read.append(
                jnp.where(near < -0.25, jnp.where(near < -0.75, reverse, both - reverse), pulled)
            )
            if with_mass:
                share = jnp.minimum(jnp.maximum(own + near, 0.0), 1.0)
                moved = share * (pulled - reverse)
                exchanged = moved if exchanged is None else exchanged + moved
        density = density + (read[component] + read[component + 1])
        add_momentum(totals, direction, read[component] - read[component + 1])
    return read, density, totals, exchanged


def relax(read, density, totals, put):
    speed = [totals[0], totals[1], totals[2] - relax_time * gravity]
    speed_square = speed[0] * speed[0] + speed[1] * speed[1] + speed[2] * speed[2]
    base = density - 1.5 * speed_square
    gain = 1.0 / relax_time
    keep = 1.0 - gain
    put(0, (gain * weight_table[0]) * base + keep * read[0])
    base_of = {1.0 / 18.0: base * (gain / 18.0), 1.0 / 36.0: base * (gain / 36.0)}
    for component in range(1, 19, 2):
        weight = weight_table[component]
        projection = dot3(velocity_table[component], speed)
        even = base_of[weight] + (4.5 * gain * weight) * (projection * projection)
        odd = (3.0 * gain * weight) * projection
        put(component, (even + odd) + keep * read[component])
        put(component + 1, (even - odd) + keep * read[component + 1])


def momentum_after(totals):
    return [totals[0], totals[1], totals[2] - gravity]


def rolled(block, shift):
    shift = shift % NZ
    return block if shift == 0 else pltpu.roll(block, shift, block.ndim - 1)


def slab_shift(direction):
    return DEEP * direction[0] + direction[2]


def slab_version(direction):
    return 3 * (direction[0] + 1) + direction[2] + 1


def kernel(
    gx_count,
    gy_count,
    pops_in,
    flags_in,
    fill_in,
    tile_in,
    weights_in,
    pops_out,
    mass_out,
    loads_out,
    streamed,
    resident,
    phases,
    current,
    mass,
    flags,
    fill,
    weights_packed,
    weights,
    y_send,
    y_recv,
    corner_recv,
    hy_send,
    hy_recv,
    hcorner_send,
    hcorner_recv,
    tile_send,
    tile_recv,
    index_block,
    index_scalars,
    slab,
    slab_resident,
    slab_streamed,
    slab_phases,
    slab_current,
    slab_deck,
    x_pack,
    y_pack,
    corner_pack,
    x_pack_recv,
    y_pack_recv,
    corner_pack_recv,
    tile_scalars,
    partial,
    first,
    second_send,
    second_recv,
    third_send,
    third_recv,
    local_sem,
    halo_send_sem,
    halo_recv_sem,
    route_send_sem,
    route_recv_sem,
):
    gx = lax.axis_index("gx")
    gy = lax.axis_index("gy")
    group_count = gx_count // 2
    member_count = 2 * gy_count
    group = gx // 2
    core = lax.rem(gx, 2)
    member = core * gy_count + gy
    east = lax.rem(gx + 1, gx_count)
    west = lax.rem(gx + gx_count - 1, gx_count)
    north = lax.rem(gy + 1, gy_count)
    south = lax.rem(gy + gy_count - 1, gy_count)

    def member_device(shift):
        other = lax.rem(member + shift, member_count)
        return other, (2 * group + other // gy_count, lax.rem(other, gy_count))

    def group_device(shift):
        other = lax.rem(group + shift, group_count)
        return other, (2 * other + lax.rem(gx, 2), gy)

    neighbours = (
        (east, gy),
        (west, gy),
        (gx, north),
        (gx, south),
        (east, north),
        (west, south),
        (east, south),
        (west, north),
    )

    loads_of = [
        pltpu.make_async_copy(flags_in, flags, local_sem.at[0]),
        pltpu.make_async_copy(fill_in, fill, local_sem.at[1]),
        pltpu.make_async_copy(pops_in, resident.at[0], local_sem.at[2]),
        pltpu.make_async_copy(weights_in, weights_packed, local_sem.at[3]),
        pltpu.make_async_copy(tile_in, tile_scalars, local_sem.at[8]),
    ]
    for copy in loads_of:
        copy.start()

    barrier = pltpu.get_barrier_semaphore()
    for device in neighbours:
        pl.semaphore_signal(barrier, inc=1, device_id=device, device_id_type=MESH)
    for shift in range(1, member_count):
        pl.semaphore_signal(
            barrier, inc=1, device_id=member_device(shift)[1], device_id_type=MESH
        )
    for shift in range(1, group_count):
        pl.semaphore_signal(
            barrier, inc=1, device_id=group_device(shift)[1], device_id_type=MESH
        )

    lane = lax.broadcasted_iota(jnp.int32, (8, NZ), 1)

    def put_phase(step, rows, code):
        phases[step, 0, rows, :] = code
        phases[step, 1, rows, :] = jnp.where(lane == 0, WALL, turned(code, 1))
        phases[step, 2, rows, :] = jnp.where(lane == NZ - 1, GAS, turned(code, -1))

    loads_of[0].wait()
    loads_of[1].wait()

    def code_rows(index, carry):
        x = index // 2
        half = remainder(index, 2)
        cells = pl.ds(aligned(8 * index, 8), 8)
        rows = pl.ds(aligned(PITCH * x + 32 + 8 * half, 8), 8)
        level = 0.5 * fill[cells, :]
        for step in range(STEPS):
            kind = flags[step, cells, :]
            code = jnp.where(
                kind == 0, FLUID, jnp.where(kind == 1, level, jnp.where(kind == 2, GAS, WALL))
            )
            put_phase(step, rows, code)
        return carry

    loop(0, 2 * CX, code_rows, 2)
    for step in range(STEPS):
        hy_send[0, step] = phases[step, 0, pl.ds(row_of(0, CY - 1), CX, stride=PITCH), :]
        hy_send[1, step] = phases[step, 0, pl.ds(row_of(0, 0), CX, stride=PITCH), :]
        for place, (x, y) in enumerate(((CX - 1, CY - 1), (0, 0), (CX - 1, 0), (0, CY - 1))):
            hcorner_send[place, pl.ds(step, 1), :] = phases[step, 0, pl.ds(row_of(x, y), 1), :]

    loads_of[2].wait()

    def first_rows(index, carry):
        x = index // 2
        half = remainder(index, 2)
        cells = pl.ds(aligned(8 * index, 8), 8)
        rows = pl.ds(aligned(PITCH * x + 32 + 8 * half, 8), 8)
        totals = [None, None, None]
        for component in range(1, 19, 2):
            direction = velocity_table[component]
            along = resident[0, component, cells, :]
            against = resident[0, component + 1, cells, :]
            add_momentum(totals, direction, along - against)
            streamed[0, SLOT[component], rows, :] = turned(along, direction[2])
            streamed[0, SLOT[component + 1], rows, :] = turned(against, -direction[2])
        for axis in range(3):
            current[0, axis, cells, :] = totals[axis]
        return carry

    loop(0, 2 * CX, first_rows, 2)
    for side, (y, components) in enumerate(((CY - 1, Y_PLUS), (0, Y_MINUS))):
        for place, component in enumerate(components):
            y_send[0, side, place] = turned(
                resident[0, component, pl.ds(y, CX, stride=CY), :], velocity_table[component][2]
            )

    pl.semaphore_wait(barrier, 8 + member_count - 1 + group_count - 1)

    def remote(source, target, exchange, place, device):
        return pltpu.make_async_remote_copy(
            src_ref=source,
            dst_ref=target,
            send_sem=halo_send_sem.at[exchange, place],
            recv_sem=halo_recv_sem.at[exchange, place],
            device_id=device,
            device_id_type=MESH,
        )

    def y_copies(step):
        return [
            remote(y_send.at[step, 0, 1, pl.ds(7, 1), :], corner_recv.at[step, 0], step, 4, neighbours[4]),
            remote(y_send.at[step, 1, 1, pl.ds(0, 1), :], corner_recv.at[step, 1], step, 5, neighbours[5]),
            remote(y_send.at[step, 1, 2, pl.ds(7, 1), :], corner_recv.at[step, 2], step, 6, neighbours[6]),
            remote(y_send.at[step, 0, 2, pl.ds(0, 1), :], corner_recv.at[step, 3], step, 7, neighbours[7]),
            remote(y_send.at[step, 0], y_recv.at[step, 0], step, 2, neighbours[2]),
            remote(y_send.at[step, 1], y_recv.at[step, 1], step, 3, neighbours[3]),
        ]

    def x_copies(step):
        return [
            remote(
                streamed.at[step, pl.ds(0, 5), pl.ds(row_of(CX - 1, 0), CY), :],
                streamed.at[step, pl.ds(0, 5), pl.ds(LOW_SLAB, CY), :],
                step,
                0,
                neighbours[0],
            ),
            remote(
                streamed.at[step, pl.ds(5, 5), pl.ds(row_of(0, 0), CY), :],
                streamed.at[step, pl.ds(5, 5), pl.ds(HIGH_SLAB, CY), :],
                step,
                1,
                neighbours[1],
            ),
        ]

    def phase_copies_of(part, exchange):
        start, count = ((0, 1), (1, STEPS - 1))[part]
        steps = pl.ds(start, count)
        return [
            remote(
                phases.at[steps, 0, pl.ds(row_of(CX - 1, 0), CY), :],
                phases.at[steps, 0, pl.ds(LOW_SLAB, CY), :],
                exchange,
                0,
                neighbours[0],
            ),
            remote(
                phases.at[steps, 0, pl.ds(row_of(0, 0), CY), :],
                phases.at[steps, 0, pl.ds(HIGH_SLAB, CY), :],
                exchange,
                1,
                neighbours[1],
            ),
            remote(hy_send.at[0, steps], hy_recv.at[0, steps], exchange, 2, neighbours[2]),
            remote(hy_send.at[1, steps], hy_recv.at[1, steps], exchange, 3, neighbours[3]),
        ]

    phase_copies = [phase_copies_of(0, STEPS), phase_copies_of(1, STEPS + 2)]
    phase_copies[0] += [
        remote(
            hcorner_send.at[place], hcorner_recv.at[place], STEPS, 4 + place, neighbours[4 + place]
        )
        for place in range(4)
    ]
    halo_copies = [y_copies(step) + x_copies(step) for step in range(STEPS)]
    slab_copies = [
        remote(x_pack.at[0], x_pack_recv.at[0], STEPS + 1, 0, neighbours[0]),
        remote(x_pack.at[1], x_pack_recv.at[1], STEPS + 1, 1, neighbours[1]),
        remote(y_pack.at[0], y_pack_recv.at[0], STEPS + 1, 2, neighbours[2]),
        remote(y_pack.at[1], y_pack_recv.at[1], STEPS + 1, 3, neighbours[3]),
        remote(corner_pack.at[0], corner_pack_recv.at[0], STEPS + 1, 4, neighbours[4]),
        remote(corner_pack.at[1], corner_pack_recv.at[1], STEPS + 1, 5, neighbours[5]),
        remote(corner_pack.at[2], corner_pack_recv.at[2], STEPS + 1, 6, neighbours[6]),
        remote(corner_pack.at[3], corner_pack_recv.at[3], STEPS + 1, 7, neighbours[7]),
    ]
    for copy in halo_copies[0]:
        copy.start()
    for copy in phase_copies[0]:
        copy.start()

    lane4 = lax.broadcasted_iota(jnp.int32, (4, NZ), 1)

    def into_slab(block_of):
        gathered = None
        for x in range(CX):
            block = rolled(block_of(x), DEEP * (x + WIDE))
            gathered = block if x == 0 else jnp.where(lane >= DEEP * (x + WIDE), block, gathered)
        return gathered

    def slab_population(component, carry):
        for half in (0, 8):
            slab[component, pl.ds(WIDE + half, 8), :] = into_slab(
                lambda x: resident[0, component, pl.ds(CY * x + half, 8), :]
            )
        return carry

    def slab_phase(step, carry):
        for half in (0, 8):
            slab[19 + step, pl.ds(WIDE + half, 8), :] = into_slab(
                lambda x: phases[step, 0, pl.ds(row_of(x, half), 8), :]
            )
        return carry

    loop(0, 19, slab_population, 19)
    loop(0, STEPS, slab_phase, STEPS)
    slab[FIELDS - 1] = jnp.zeros((SLAB_ROWS, NZ), F32)

    def pack(part, carry):
        for half in (0, 1):
            blocks = [slab[4 * part + j, pl.ds(WIDE + 8 * half, 8), :] for j in range(4)]
            for side, start in ((0, 64), (1, 32)):
                packed = rolled(blocks[0], -start)
                for j in (1, 2, 3):
                    packed = jnp.where(lane >= 32 * j, rolled(blocks[j], 32 * j - start), packed)
                x_pack[side, part, pl.ds(8 * half, 8), :] = packed
            for j in (0, 1):
                packed = jnp.where(
                    lane < 64, rolled(blocks[2 * j], -32), rolled(blocks[2 * j + 1], 32)
                )
                if half == 1:
                    y_pack[0, part, pl.ds(4 * j, 4), :] = packed[4:8, :]
                else:
                    y_pack[1, part, pl.ds(4 * j, 4), :] = packed[0:4, :]
        return carry

    loop(0, FIELDS // 4, pack, FIELDS // 4)
    for part in range(FIELDS // 4):
        rows = pl.ds(4 * (part % 2), 4)
        corner_pack[0, part // 2, rows, :] = x_pack[0, part, pl.ds(12, 4), :]
        corner_pack[1, part // 2, rows, :] = x_pack[1, part, pl.ds(0, 4), :]
        corner_pack[2, part // 2, rows, :] = x_pack[0, part, pl.ds(0, 4), :]
        corner_pack[3, part // 2, rows, :] = x_pack[1, part, pl.ds(12, 4), :]
    for copy in slab_copies:
        copy.start()
    for copy in phase_copies[1]:
        copy.start()

    loads_of[4].wait()
    tile_send[...] = jnp.where(
        lane == 2 * member,
        tile_scalars[0, 0],
        jnp.where(lane == 2 * member + 1, tile_scalars[0, 1], 0),
    )
    tile_recv[member] = tile_send[...]

    def route(source, target, kind, device):
        return pltpu.make_async_remote_copy(
            src_ref=source,
            dst_ref=target,
            send_sem=route_send_sem.at[kind],
            recv_sem=route_recv_sem.at[kind],
            device_id=device,
            device_id_type=MESH,
        )

    def wait_bytes(ref, semaphore):
        pltpu.make_async_copy(ref, ref, semaphore).wait()

    def tell_members(shift, carry):
        route(tile_send, tile_recv.at[member], 0, member_device(shift)[1]).start()
        return carry

    lax.fori_loop(1, member_count, tell_members, 0)

    def update(step, prow, crow, column=None):
        final = step == STEPS - 1
        pstep, cstep = (PITCH, CY) if column is not None else (None, None)

        def rows(offset):
            if pstep is None:
                return pl.ds(prow + offset, 8)
            return pl.ds(prow + offset, 8, stride=pstep)

        cells = pl.ds(crow, 8) if cstep is None else pl.ds(crow, 8, stride=cstep)
        own = phases[step, 0, rows(0), :]
        liquid = own > -0.25
        offsets = [PITCH * direction[0] + direction[1] for direction in velocity_table]
        read, density, totals, exchanged = gather(
            own,
            [current[step, axis, cells, :] for axis in range(3)],
            lambda component: resident[step, component, cells, :],
            lambda component: streamed[step, SLOT[component], rows(-offsets[component]), :],
            lambda component: phases[
                step, version_of(velocity_table[component][2]), rows(-offsets[component]), :
            ],
            True,
        )
        interface = jnp.logical_and(liquid, own < 0.75)
        exchanged = jnp.where(interface, exchanged, 0.0)
        if step > 0:
            exchanged = exchanged + mass[step - 1, cells, :]
        if final:
            mass_out[cells, :] = exchanged
        else:
            mass[step, cells, :] = exchanged

        def put(component, value):
            value = jnp.where(liquid, value, weight_table[component])
            if final:
                pops_out[component, cells, :] = value
                return
            resident[step + 1, component, cells, :] = value
            if component == 0:
                return
            value = turned(value, velocity_table[component][2])
            streamed[step + 1, SLOT[component], rows(0), :] = value
            if column is not None:
                side, names = (0, Y_PLUS) if column > 0 else (1, Y_MINUS)
                if component in names:
                    y_send[step + 1, side, names.index(component)] = value

        relax(read, density, totals, put)
        if not final:
            for axis, value in enumerate(momentum_after(totals)):
                current[step + 1, axis, cells, :] = jnp.where(liquid, value, 0.0)

    def interior(step):
        def slab(x, carry):
            for y in (1, 7):
                update(step, PITCH * x + PITCH + 8 + y, CY * x + y)
            return carry

        loop(1, CX - 1, slab, 1)

    def y_border(step):
        for y in (0, CY - 1):
            update(step, row_of(0, y), y, column=y)

    def x_border(step):
        def slab(index, carry):
            x = (CX - 1) * (index // 2)
            half = 8 * remainder(index, 2)
            update(
                step,
                aligned(PITCH * x + PITCH + 8 + half, 8),
                aligned(CY * x + half, 8),
            )
            return carry

        loop(0, 4, slab, 4)

    corners = (
        (7, row_of(-1, -1), CX - 1),
        (8, row_of(CX, CY), 0),
        (9, row_of(-1, CY), CX - 1),
        (10, row_of(CX, -1), 0),
    )

    def unpack(step):
        for copy in halo_copies[step]:
            copy.wait_recv()
        for side, (y, names) in enumerate(((-1, Y_PLUS), (CY, Y_MINUS))):
            for place, component in enumerate(names):
                streamed[step, SLOT[component], pl.ds(row_of(0, y), CX, stride=PITCH), :] = y_recv[
                    step, side, place
                ]
        for place, (component, row, x) in enumerate(corners):
            streamed[step, SLOT[component], pl.ds(row, 1), :] = corner_recv[step, place]

    def unpack_phases(part):
        for copy in phase_copies[part]:
            copy.wait_recv()
        at_west, at_east = gx == 0, gx == gx_count - 1
        at_south, at_north = gy == 0, gy == gy_count - 1

        def one(step, carry):
            for start, edge in ((LOW_SLAB, at_west), (HIGH_SLAB, at_east)):
                for half in (0, 8):
                    rows = pl.ds(start + half, 8)
                    put_phase(step, rows, jnp.where(edge, GAS, phases[step, 0, rows, :]))
            for side, (y, edge) in enumerate(((-1, at_south), (CY, at_north))):
                rows = pl.ds(row_of(0, y), CX, stride=PITCH)
                put_phase(step, rows, jnp.where(edge, GAS, hy_recv[side, step]))
            edges = (
                at_west | at_south,
                at_east | at_north,
                at_west | at_north,
                at_east | at_south,
            )
            for place, (component, row, x) in enumerate(corners):
                code = hcorner_recv[place, pl.ds(step, 1), :]
                phases[step, 0, pl.ds(row, 1), :] = jnp.where(edges[place], GAS, code)
            return carry

        loop(*((0, 1), (1, STEPS))[part], one, STEPS)

    def find_tiles():
        wait_bytes(tile_recv.at[pl.ds(0, member_count - 1)], route_recv_sem.at[0])
        names = tile_recv[0]
        for place in range(1, member_count):
            names = names + tile_recv[place]
        sublane = lax.broadcasted_iota(jnp.int32, (8, NZ), 0)
        none = 2 * member_count
        lasts = earlies = jnp.zeros((8, NZ), jnp.int32)
        for place in range(group_count):
            wanted = (2 * place + core) * gy_count + sublane
            match = jnp.logical_and(names == wanted, lane < none)
            last = jnp.max(jnp.where(match, lane, -1), axis=1, keepdims=True)
            early = jnp.min(jnp.where(match, lane, none), axis=1, keepdims=True)
            early = jnp.where(early == last, none, early)
            last = jnp.where(last < 0, none, last)
            lasts = jnp.where(lane == place, last, lasts)
            earlies = jnp.where(lane == place, early, earlies)
        index_block[0] = lasts
        index_block[1] = earlies
        copy = pltpu.make_async_copy(index_block, index_scalars, local_sem.at[4])
        copy.start()
        copy.wait()

    def widen_weights():
        loads_of[3].wait()
        for part in range(CELLS // 16):
            rows = pl.ds(16 * part, 16)
            weights[rows, :] = weights_packed[rows, :].astype(F32)

    def unpack_slab():
        for copy in slab_copies:
            copy.wait_recv()

        def fields(part, carry):
            quarter = pl.ds(4 * remainder(part, 2), 4)
            for j in range(4):
                field = 4 * part + j
                for half in (0, 8):
                    rows = pl.ds(WIDE + half, 8)
                    low = rolled(x_pack_recv[0, part, pl.ds(half, 8), :], -32 * j)
                    high = rolled(x_pack_recv[1, part, pl.ds(half, 8), :], 96 - 32 * j)
                    slab[field, rows, :] = jnp.where(
                        lane < 32, low, jnp.where(lane >= 96, high, slab[field, rows, :])
                    )
                for side, row, west_corner, east_corner in ((0, 0, 0, 3), (1, CY + WIDE, 2, 1)):
                    middle = rolled(
                        y_pack_recv[side, part, pl.ds(4 * (j // 2), 4), :], 32 - 64 * (j % 2)
                    )
                    low = rolled(corner_pack_recv[west_corner, part // 2, quarter, :], -32 * j)
                    high = rolled(corner_pack_recv[east_corner, part // 2, quarter, :], 96 - 32 * j)
                    slab[field, pl.ds(row, 4), :] = jnp.where(
                        lane4 < 32, low, jnp.where(lane4 >= 96, high, middle)
                    )
            return carry

        loop(0, FIELDS // 4, fields, 6)
        low_lane = jnp.where(gx == 0, DEEP * WIDE, 0)
        high_lane = jnp.where(gx == gx_count - 1, NZ - DEEP * WIDE, NZ)
        low_row = jnp.where(gy == 0, WIDE, 0)
        high_row = jnp.where(gy == gy_count - 1, CY + WIDE, SLAB_ROWS)
        level = lax.rem(lane, DEEP)

        def ready(block, carry):
            start = aligned(8 * block, 8)
            cells = pl.ds(start, 8)
            rows = pl.ds(aligned(start + 8, 8), 8)
            totals = [None, None, None]
            for component in range(1, 19, 2):
                direction = velocity_table[component]
                along = slab[component, cells, :]
                against = slab[component + 1, cells, :]
                add_momentum(totals, direction, along - against)
                shift = slab_shift(direction)
                slab_streamed[0, SLOT[component], rows, :] = rolled(along, shift)
                slab_streamed[0, SLOT[component + 1], rows, :] = rolled(against, -shift)
            for axis in range(3):
                slab_current[0, axis, cells, :] = totals[axis]
            row = lax.broadcasted_iota(jnp.int32, (8, NZ), 0) + start
            inside = jnp.logical_and(
                jnp.logical_and(lane >= low_lane, lane < high_lane),
                jnp.logical_and(row >= low_row, row < high_row),
            )
            for step in range(STEPS):
                code = jnp.where(inside, slab[19 + step, cells, :], GAS)
                for shift_x in (-1, 0, 1):
                    for shift_z in (-1, 0, 1):
                        direction = (shift_x, 0, shift_z)
                        value = rolled(code, slab_shift(direction))
                        if shift_z == 1:
                            value = jnp.where(level == 0, WALL, value)
                        slab_phases[step, slab_version(direction), rows, :] = value
            return carry

        loop(0, SLAB_ROWS // 8, ready, 3)

    def slab_update(step, start):
        cells = pl.ds(start, 8)

        def rows(offset):
            return pl.ds(start + 8 + offset, 8)

        def own_of(component):
            if step == 0:
                return slab[component, cells, :]
            return slab_resident[step - 1, component, cells, :]

        own = slab_phases[step, slab_version((0, 0, 0)), rows(0), :]
        liquid = own > -0.25
        read, density, totals, _ = gather(
            own,
            [slab_current[step, axis, cells, :] for axis in range(3)],
            own_of,
            lambda component: slab_streamed[
                step, SLOT[component], rows(-velocity_table[component][1]), :
            ],
            lambda component: slab_phases[
                step,
                slab_version(velocity_table[component]),
                rows(-velocity_table[component][1]),
                :,
            ],
            False,
        )
        slab_deck[step, cells, :] = jnp.where(liquid, density * (1.0 / 3.0), 0.0)
        if step == STEPS - 1:
            return

        def put(component, value):
            value = jnp.where(liquid, value, weight_table[component])
            slab_resident[step, component, cells, :] = value
            if component > 0:
                slab_streamed[step + 1, SLOT[component], rows(0), :] = rolled(
                    value, slab_shift(velocity_table[component])
                )

        relax(read, density, totals, put)
        for axis, value in enumerate(momentum_after(totals)):
            slab_current[step + 1, axis, cells, :] = jnp.where(liquid, value, 0.0)

    def slab_steps():
        for step in range(STEPS - 1):

            def block(index, carry, step=step):
                slab_update(step, aligned(8 * index, 8))
                return carry

            loop(0, SLAB_ROWS // 8, block, 3)
        for start in (WIDE, WIDE + 8):
            slab_update(STEPS - 1, start)

    def first_leg():
        def one(step, carry):
            for tile in range(2):
                sums = [None] * 8
                for part in range(8):
                    x = 4 * tile + part // 2
                    cells = pl.ds(64 * tile + 8 * part, 8)
                    pressure = slab_deck[step, pl.ds(WIDE + 8 * (part % 2), 8), :]
                    pressure = pressure.astype(jnp.bfloat16).astype(F32)
                    place = DEEP * (x + WIDE)
                    pressure = jnp.broadcast_to(pressure[:, place : place + 1], (8, NZ))
                    for column in range(8):
                        term = pressure * weights[cells, pl.ds(NZ * column, NZ)]
                        sums[column] = term if part == 0 else sums[column] + term
                for column in range(8):
                    partial[column, tile, pl.ds(step, 1), :] = jnp.sum(
                        sums[column], axis=0, keepdims=True
                    )
            return carry

        loop(0, STEPS, one, 2)
        for tile in range(2):
            first[2 * member + tile] = partial[gy, tile]

        def send(shift, carry):
            other, device = member_device(shift)
            route(
                partial.at[lax.rem(other, gy_count)],
                first.at[pl.ds(2 * member, 2)],
                1,
                device,
            ).start()
            return carry

        lax.fori_loop(1, member_count, send, 0)

    def second_leg():
        wait_bytes(first.at[pl.ds(0, 2 * (member_count - 1))], route_recv_sem.at[1])

        def owners(place, carry):
            for y in range(gy_count):
                second_send[place, y] = (
                    first[index_scalars[0, y, place]] + first[index_scalars[1, y, place]]
                )
            return carry

        loop(0, group_count, owners, 4)
        second_recv[group] = second_send[group]

        def send(shift, carry):
            other, device = group_device(shift)
            route(second_send.at[other], second_recv.at[group], 2, device).start()
            return carry

        lax.fori_loop(1, group_count, send, 0)

    def third_leg():
        wait_bytes(second_recv.at[pl.ds(0, group_count - 1)], route_recv_sem.at[2])
        for y in range(gy_count):
            total = second_recv[0, y]
            for place in range(1, group_count):
                total = total + second_recv[place, y]
            third_send[y] = total
        third_recv[gy] = third_send[gy]

        def send(shift, carry):
            other = lax.rem(gy + shift, gy_count)
            route(third_send.at[other], third_recv.at[gy], 3, (gx, other)).start()
            return carry

        lax.fori_loop(1, gy_count, send, 0)

    def collect():
        wait_bytes(third_recv.at[pl.ds(0, gy_count - 1)], route_recv_sem.at[3])
        for y in range(gy_count):
            loads_out[:, pl.ds(NZ * y, NZ)] = third_recv[y]

    first[2 * member_count] = jnp.zeros((STEPS, NZ), F32)

    for step in range(STEPS):
        if step == 0:
            widen_weights()
            interior(step)
            find_tiles()
            unpack_phases(0)
        if step == 1:
            unpack_slab()
            slab_steps()
            first_leg()
            interior(step)
            unpack_phases(1)
        if step == 2:
            interior(step)
            second_leg()
        if step == 3:
            interior(step)
            third_leg()
        unpack(step)
        y_border(step)
        if step < STEPS - 1:
            for copy in halo_copies[step + 1][:6]:
                copy.start()
        x_border(step)
        if step < STEPS - 1:
            for copy in halo_copies[step + 1][6:]:
                copy.start()

    collect()
    for copies in phase_copies:
        for copy in copies:
            copy.wait_send()
    for copy in slab_copies:
        copy.wait_send()
    for copies in halo_copies:
        for copy in copies:
            copy.wait_send()
    wait_bytes(tile_recv.at[pl.ds(0, member_count - 1)], route_send_sem.at[0])
    wait_bytes(first.at[pl.ds(0, 2 * (member_count - 1))], route_send_sem.at[1])
    wait_bytes(second_send.at[pl.ds(0, group_count - 1)], route_send_sem.at[2])
    wait_bytes(third_send.at[pl.ds(0, gy_count - 1)], route_send_sem.at[3])


def hand_over(pops, mass, loads, pops_out, mass_out, loads_out, semaphores):
    copies = [
        pltpu.make_async_copy(pops, pops_out, semaphores.at[0]),
        pltpu.make_async_copy(mass, mass_out, semaphores.at[1]),
        pltpu.make_async_copy(loads, loads_out, semaphores.at[2]),
    ]
    for copy in copies:
        copy.start()
    for copy in copies:
        copy.wait()


def per_device(gx_count, gy_count, populations, cell_flags, fill_level, tile_block, deck_weights):
    members, groups = 2 * gy_count, gx_count // 2
    whole = pl.BlockSpec(memory_space=pltpu.HBM)
    keep = pl.BlockSpec(memory_space=pl.ANY)
    placed = functools.partial(pltpu.with_memory_space_constraint, memory_space=pltpu.HBM)
    pops, mass, loads = pl.pallas_call(
        functools.partial(kernel, gx_count, gy_count),
        out_shape=(
            pltpu.VMEM((19, CELLS, NZ), F32),
            pltpu.VMEM((CELLS, NZ), F32),
            pltpu.VMEM((STEPS, 1024), F32),
        ),
        in_specs=[whole] * 5,
        out_specs=(pl.BlockSpec(memory_space=pltpu.VMEM),) * 3,
        scratch_shapes=[
            pltpu.VMEM((STEPS, 18, ROWS, NZ), F32),
            pltpu.VMEM((STEPS, 19, CELLS, NZ), F32),
            pltpu.VMEM((STEPS, 3, ROWS, NZ), F32),
            pltpu.VMEM((STEPS, 3, CELLS, NZ), F32),
            pltpu.VMEM((STEPS - 1, CELLS, NZ), F32),
            pltpu.VMEM((STEPS, CELLS, NZ), jnp.int32),
            pltpu.VMEM((CELLS, NZ), F32),
            pltpu.VMEM((CELLS, 1024), jnp.bfloat16),
            pltpu.VMEM((CELLS, 1024), F32),
            pltpu.VMEM((STEPS, 2, 5, 8, NZ), F32),
            pltpu.VMEM((STEPS, 2, 5, 8, NZ), F32),
            pltpu.VMEM((STEPS, 4, 1, NZ), F32),
            pltpu.VMEM((2, STEPS, 8, NZ), F32),
            pltpu.VMEM((2, STEPS, 8, NZ), F32),
            pltpu.VMEM((4, STEPS, NZ), F32),
            pltpu.VMEM((4, STEPS, NZ), F32),
            pltpu.VMEM((8, NZ), jnp.int32),
            pltpu.VMEM((members, 8, NZ), jnp.int32),
            pltpu.VMEM((2, 8, NZ), jnp.int32),
            pltpu.SMEM((2, 8, NZ), jnp.int32),
            pltpu.VMEM((FIELDS, SLAB_ROWS, NZ), F32),
            pltpu.VMEM((STEPS - 1, 19, SLAB_ROWS, NZ), F32),
            pltpu.VMEM((STEPS, 18, SLAB_ROWS + 16, NZ), F32),
            pltpu.VMEM((STEPS, 9, SLAB_ROWS + 16, NZ), F32),
            pltpu.VMEM((STEPS, 3, SLAB_ROWS, NZ), F32),
            pltpu.VMEM((STEPS, SLAB_ROWS, NZ), F32),
            pltpu.VMEM((2, FIELDS // 4, CY, NZ), F32),
            pltpu.VMEM((2, FIELDS // 4, 8, NZ), F32),
            pltpu.VMEM((4, FIELDS // 8, 8, NZ), F32),
            pltpu.VMEM((2, FIELDS // 4, CY, NZ), F32),
            pltpu.VMEM((2, FIELDS // 4, 8, NZ), F32),
            pltpu.VMEM((4, FIELDS // 8, 8, NZ), F32),
            pltpu.SMEM((1, 2), jnp.int32),
            pltpu.VMEM((8, 2, STEPS, NZ), F32),
            pltpu.VMEM((2 * members + 1, STEPS, NZ), F32),
            pltpu.VMEM((groups, gy_count, STEPS, NZ), F32),
            pltpu.VMEM((groups, gy_count, STEPS, NZ), F32),
            pltpu.VMEM((gy_count, STEPS, NZ), F32),
            pltpu.VMEM((gy_count, STEPS, NZ), F32),
            pltpu.SemaphoreType.DMA((9,)),
            pltpu.SemaphoreType.DMA((STEPS + 3, 8)),
            pltpu.SemaphoreType.DMA((STEPS + 3, 8)),
            pltpu.SemaphoreType.DMA((4,)),
            pltpu.SemaphoreType.DMA((4,)),
        ],
        compiler_params=pltpu.CompilerParams(
            collective_id=0, has_side_effects=True, vmem_limit_bytes=32 * 1024 * 1024
        ),
    )(
        placed(populations.reshape(19, CELLS, NZ)),
        placed(cell_flags.reshape(STEPS, CELLS, NZ)),
        placed(fill_level.reshape(CELLS, NZ)),
        placed(tile_block.reshape(1, 2)),
        placed(deck_weights.reshape(CELLS, 1024)),
    )
    pops, mass, loads = pl.pallas_call(
        hand_over,
        out_shape=(
            pltpu.HBM((19, CELLS, NZ), F32),
            pltpu.HBM((CELLS, NZ), F32),
            pltpu.HBM((STEPS, 1024), F32),
        ),
        in_specs=[keep] * 3,
        out_specs=(whole, whole, whole),
        scratch_shapes=[pltpu.SemaphoreType.DMA((3,))],
    )(*(pltpu.with_memory_space_constraint(part, pltpu.VMEM) for part in (pops, mass, loads)))
    return (
        pops.reshape(19, CX, CY, NZ),
        mass.reshape(CX, CY, NZ),
        loads.reshape(1, STEPS, 1024),
    )


def solution(mesh):
    placed = (
        P(None, "gx", "gy", None),
        P(None, "gx", "gy", None),
        P("gx", "gy", None),
        P("gx", "gy"),
        P("gx", "gy", None, None),
    )
    return jax.shard_map(
        functools.partial(per_device, mesh.shape["gx"], mesh.shape["gy"]),
        mesh=mesh,
        in_specs=placed,
        out_specs=(P(None, "gx", "gy", None), P("gx", "gy", None), P(("gx", "gy"), None, None)),
        check_vma=False,
    )
```

```python
import functools

import jax
import jax.numpy as jnp
from jax import lax
from jax.experimental import pallas as pl
from jax.experimental.pallas import tpu as pltpu
from jax.sharding import PartitionSpec as P

velocity_table = (
    (0, 0, 0),
    (1, 0, 0),
    (-1, 0, 0),
    (0, 1, 0),
    (0, -1, 0),
    (0, 0, 1),
    (0, 0, -1),
    (1, 1, 0),
    (-1, -1, 0),
    (1, -1, 0),
    (-1, 1, 0),
    (1, 0, 1),
    (-1, 0, -1),
    (1, 0, -1),
    (-1, 0, 1),
    (0, 1, 1),
    (0, -1, -1),
    (0, 1, -1),
    (0, -1, 1),
)
weight_table = (1.0 / 3.0,) + (1.0 / 18.0,) * 6 + (1.0 / 36.0,) * 12
relax_time = 0.8
gravity = 0.001

MESH = pl.DeviceIdType.MESH
F32 = jnp.float32
STEPS = 4
CX, CY, NZ = 8, 16, 128
CELLS = CX * CY
PITCH = 24
ROWS = 248
LOW_SLAB = 8
HIGH_SLAB = PITCH * (CX + 1) + 8
X_PLUS = (1, 7, 9, 11, 13)
X_MINUS = (2, 8, 10, 12, 14)
Y_PLUS = (3, 7, 10, 15, 17)
Y_MINUS = (4, 8, 9, 16, 18)
SLOTS = X_PLUS + X_MINUS + (3, 4, 5, 6, 15, 16, 17, 18)
SLOT = {component: place for place, component in enumerate(SLOTS)}
DEEP, WIDE = 8, 4
SLAB_ROWS = CY + 2 * WIDE
FIELDS = 24
Z_HIGH, Z_LOW, Y_COUNT = 4, 2, 4
Z_COUNT = Z_HIGH * Z_LOW
FLUID, GAS, WALL = 1.0, -0.5, -1.0


def aligned(value, unit):
    return value if isinstance(value, int) else pl.multiple_of(value, unit)


def remainder(value, unit):
    return value % unit if isinstance(value, int) else lax.rem(value, unit)


def loop(low, high, body, group):
    if group >= high - low:
        for index in range(low, high):
            body(index, 0)
        return
    turns = (high - low) // group

    def turn(index, carry):
        for place in range(group):
            body(low + index * group + place, 0)
        return carry

    lax.fori_loop(0, turns, turn, 0)


def row_of(x, y):
    return PITCH * (x + 1) + 8 + y


def turned(block, shift):
    if shift == 0:
        return block
    return pltpu.roll(block, shift % NZ, block.ndim - 1)


def version_of(shift_z):
    return 0 if shift_z == 0 else (1 if shift_z == 1 else 2)


def dot3(direction, vector):
    result = None
    for factor, part in zip(direction, vector):
        if factor == 0:
            continue
        if result is None:
            result = part if factor > 0 else -part
        else:
            result = result + part if factor > 0 else result - part
    return result


def add_momentum(totals, direction, difference):
    for axis, factor in enumerate(direction):
        if factor == 0:
            continue
        if totals[axis] is None:
            totals[axis] = difference if factor > 0 else -difference
        elif factor > 0:
            totals[axis] = totals[axis] + difference
        else:
            totals[axis] = totals[axis] - difference


def gather(own, flow, resident, pulled_of, near_of, with_mass):
    flow_square = flow[0] * flow[0] + flow[1] * flow[1] + flow[2] * flow[2]
    rest = 1.0 - 1.5 * flow_square
    rest_of = {1.0 / 18.0: rest * (2.0 / 18.0), 1.0 / 36.0: rest * (2.0 / 36.0)}
    density = resident(0)
    read = [density]
    totals = [None, None, None]
    exchanged = None
    for component in range(1, 19, 2):
        direction = velocity_table[component]
        weight = weight_table[component]
        projection = dot3(direction, flow)
        both = rest_of[weight] + (9.0 * weight) * (projection * projection)
        along = resident(component)
        against = resident(component + 1)
        for place, reverse in ((component, against), (component + 1, along)):
            pulled = pulled_of(place)
            near = near_of(place)
            read.append(
                jnp.where(near < -0.25, jnp.where(near < -0.75, reverse, both - reverse), pulled)
            )
            if with_mass:
                share = jnp.minimum(jnp.maximum(own + near, 0.0), 1.0)
                moved = share * (pulled - reverse)
                exchanged = moved if exchanged is None else exchanged + moved
        density = density + (read[component] + read[component + 1])
        add_momentum(totals, direction, read[component] - read[component + 1])
    return read, density, totals, exchanged


def relax(read, density, totals, put):
    speed = [totals[0], totals[1], totals[2] - relax_time * gravity]
    speed_square = speed[0] * speed[0] + speed[1] * speed[1] + speed[2] * speed[2]
    base = density - 1.5 * speed_square
    gain = 1.0 / relax_time
    keep = 1.0 - gain
    put(0, (gain * weight_table[0]) * base + keep * read[0])
    base_of = {1.0 / 18.0: base * (gain / 18.0), 1.0 / 36.0: base * (gain / 36.0)}
    for component in range(1, 19, 2):
        weight = weight_table[component]
        projection = dot3(velocity_table[component], speed)
        even = base_of[weight] + (4.5 * gain * weight) * (projection * projection)
        odd = (3.0 * gain * weight) * projection
        put(component, (even + odd) + keep * read[component])
        put(component + 1, (even - odd) + keep * read[component + 1])


def momentum_after(totals):
    return [totals[0], totals[1], totals[2] - gravity]


def rolled(block, shift):
    shift = shift % NZ
    return block if shift == 0 else pltpu.roll(block, shift, block.ndim - 1)


def slab_shift(direction):
    return DEEP * direction[0] + direction[2]


def slab_version(direction):
    return 3 * (direction[0] + 1) + direction[2] + 1


def kernel(
    gx_count,
    gy_count,
    pops_in,
    flags_in,
    fill_in,
    tile_in,
    weights_in,
    pops_out,
    mass_out,
    loads_out,
    streamed,
    resident,
    phases,
    current,
    mass,
    flags,
    fill,
    weights_packed,
    weights,
    y_send,
    y_recv,
    corner_recv,
    hy_send,
    hy_recv,
    hcorner_send,
    hcorner_recv,
    tile_send,
    tile_recv,
    index_block,
    index_scalars,
    slab,
    slab_resident,
    slab_streamed,
    slab_phases,
    slab_current,
    slab_deck,
    x_pack,
    y_pack,
    corner_pack,
    x_pack_recv,
    y_pack_recv,
    corner_pack_recv,
    tile_scalars,
    partial,
    first,
    second_send,
    second_recv,
    third_send,
    third_recv,
    local_sem,
    halo_send_sem,
    halo_recv_sem,
    route_send_sem,
    route_recv_sem,
):
    gx = lax.axis_index("gx")
    gy = lax.axis_index("gy")
    group_count, member_count = Y_COUNT * (gx_count // (2 * Z_HIGH)), 2 * Z_COUNT
    core = lax.rem(gx, 2)
    chip_x, chip_y = gx // (2 * Z_HIGH), gy // Z_LOW
    chip_z = Z_LOW * lax.rem(gx // 2, Z_HIGH) + lax.rem(gy, Z_LOW)
    group = chip_x * Y_COUNT + chip_y
    member = core * Z_COUNT + chip_z

    def device_of(place_x, place_y, place_z, place_core):
        return (
            (place_x * Z_HIGH + place_z // Z_LOW) * 2 + place_core,
            place_y * Z_LOW + lax.rem(place_z, Z_LOW),
        )

    east = lax.rem(gx + 1, gx_count)
    west = lax.rem(gx + gx_count - 1, gx_count)
    north = lax.rem(gy + 1, gy_count)
    south = lax.rem(gy + gy_count - 1, gy_count)

    def member_device(shift):
        shift_z, shift_core = shift
        other_z = lax.rem(chip_z + shift_z, Z_COUNT)
        return other_z, device_of(chip_x, chip_y, other_z, lax.rem(core + shift_core, 2))

    def group_device(shift):
        other_x = lax.rem(chip_x + shift[0], group_count // Y_COUNT)
        other_y = lax.rem(chip_y + shift[1], Y_COUNT)
        return other_x * Y_COUNT + other_y, device_of(other_x, other_y, chip_z, core)

    def ring(shift, count):
        return min(shift, count - shift)

    z_shifts = sorted(range(1, Z_COUNT), key=lambda shift: -ring(shift, Z_COUNT))
    member_shifts = [(shift, flip) for shift in z_shifts for flip in (0, 1)] + [(0, 1)]
    x_count = group_count // Y_COUNT
    group_shifts = sorted(
        [(i, j) for i in range(x_count) for j in range(Y_COUNT) if i or j],
        key=lambda shift: -(ring(shift[0], x_count) + ring(shift[1], Y_COUNT)),
    )

    neighbours = (
        (east, gy),
        (west, gy),
        (gx, north),
        (gx, south),
        (east, north),
        (west, south),
        (east, south),
        (west, north),
    )

    loads_of = [
        pltpu.make_async_copy(flags_in, flags, local_sem.at[0]),
        pltpu.make_async_copy(fill_in, fill, local_sem.at[1]),
        pltpu.make_async_copy(pops_in, resident.at[0], local_sem.at[2]),
        pltpu.make_async_copy(weights_in, weights_packed, local_sem.at[3]),
        pltpu.make_async_copy(tile_in, tile_scalars, local_sem.at[8]),
    ]
    for copy in loads_of:
        copy.start()

    barrier = pltpu.get_barrier_semaphore()
    for device in neighbours:
        pl.semaphore_signal(barrier, inc=1, device_id=device, device_id_type=MESH)
    for shift in member_shifts:
        pl.semaphore_signal(
            barrier, inc=1, device_id=member_device(shift)[1], device_id_type=MESH
        )
    for shift in group_shifts:
        pl.semaphore_signal(
            barrier, inc=1, device_id=group_device(shift)[1], device_id_type=MESH
        )

    lane = lax.broadcasted_iota(jnp.int32, (8, NZ), 1)

    def put_phase(step, rows, code):
        phases[step, 0, rows, :] = code
        phases[step, 1, rows, :] = jnp.where(lane == 0, WALL, turned(code, 1))
        phases[step, 2, rows, :] = jnp.where(lane == NZ - 1, GAS, turned(code, -1))

    loads_of[0].wait()
    loads_of[1].wait()

    def code_rows(index, carry):
        x = index // 2
        half = remainder(index, 2)
        cells = pl.ds(aligned(8 * index, 8), 8)
        rows = pl.ds(aligned(PITCH * x + 32 + 8 * half, 8), 8)
        level = 0.5 * fill[cells, :]
        for step in range(STEPS):
            kind = flags[step, cells, :]
            code = jnp.where(
                kind == 0, FLUID, jnp.where(kind == 1, level, jnp.where(kind == 2, GAS, WALL))
            )
            put_phase(step, rows, code)
        return carry

    loop(0, 2 * CX, code_rows, 4)
    for step in range(STEPS):
        hy_send[0, step] = phases[step, 0, pl.ds(row_of(0, CY - 1), CX, stride=PITCH), :]
        hy_send[1, step] = phases[step, 0, pl.ds(row_of(0, 0), CX, stride=PITCH), :]
        for place, (x, y) in enumerate(((CX - 1, CY - 1), (0, 0), (CX - 1, 0), (0, CY - 1))):
            hcorner_send[place, pl.ds(step, 1), :] = phases[step, 0, pl.ds(row_of(x, y), 1), :]

    loads_of[2].wait()

    def first_rows(index, carry):
        x = index // 2
        half = remainder(index, 2)
        cells = pl.ds(aligned(8 * index, 8), 8)
        rows = pl.ds(aligned(PITCH * x + 32 + 8 * half, 8), 8)
        totals = [None, None, None]
        for component in range(1, 19, 2):
            direction = velocity_table[component]
            along = resident[0, component, cells, :]
            against = resident[0, component + 1, cells, :]
            add_momentum(totals, direction, along - against)
            streamed[0, SLOT[component], rows, :] = turned(along, direction[2])
            streamed[0, SLOT[component + 1], rows, :] = turned(against, -direction[2])
        for axis in range(3):
            current[0, axis, cells, :] = totals[axis]
        return carry

    loop(0, 2 * CX, first_rows, 4)
    for side, (y, components) in enumerate(((CY - 1, Y_PLUS), (0, Y_MINUS))):
        for place, component in enumerate(components):
            y_send[0, side, place] = turned(
                resident[0, component, pl.ds(y, CX, stride=CY), :], velocity_table[component][2]
            )

    lane4 = lax.broadcasted_iota(jnp.int32, (4, NZ), 1)

    def into_slab(block_of):
        gathered = None
        for x in range(CX):
            block = rolled(block_of(x), DEEP * (x + WIDE))
            gathered = block if x == 0 else jnp.where(lane >= DEEP * (x + WIDE), block, gathered)
        return gathered

    def slab_population(component, carry):
        for half in (0, 8):
            slab[component, pl.ds(WIDE + half, 8), :] = into_slab(
                lambda x: resident[0, component, pl.ds(CY * x + half, 8), :]
            )
        return carry

    def slab_phase(step, carry):
        for half in (0, 8):
            slab[19 + step, pl.ds(WIDE + half, 8), :] = into_slab(
                lambda x: phases[step, 0, pl.ds(row_of(x, half), 8), :]
            )
        return carry

    loop(0, 19, slab_population, 19)
    loop(0, STEPS, slab_phase, 4)
    slab[FIELDS - 1] = jnp.zeros((SLAB_ROWS, NZ), F32)

    def pack(part, carry):
        for half in (0, 1):
            blocks = [slab[4 * part + j, pl.ds(WIDE + 8 * half, 8), :] for j in range(4)]
            for side, start in ((0, 64), (1, 32)):
                packed = rolled(blocks[0], -start)
                for j in (1, 2, 3):
                    packed = jnp.where(lane >= 32 * j, rolled(blocks[j], 32 * j - start), packed)
                x_pack[side, part, pl.ds(8 * half, 8), :] = packed
            for j in (0, 1):
                packed = jnp.where(
                    lane < 64, rolled(blocks[2 * j], -32), rolled(blocks[2 * j + 1], 32)
                )
                if half == 1:
                    y_pack[0, part, pl.ds(4 * j, 4), :] = packed[4:8, :]
                else:
                    y_pack[1, part, pl.ds(4 * j, 4), :] = packed[0:4, :]
        return carry

    loop(0, FIELDS // 4, pack, FIELDS // 4)
    for part in range(FIELDS // 4):
        rows = pl.ds(4 * (part % 2), 4)
        corner_pack[0, part // 2, rows, :] = x_pack[0, part, pl.ds(12, 4), :]
        corner_pack[1, part // 2, rows, :] = x_pack[1, part, pl.ds(0, 4), :]
        corner_pack[2, part // 2, rows, :] = x_pack[0, part, pl.ds(0, 4), :]
        corner_pack[3, part // 2, rows, :] = x_pack[1, part, pl.ds(12, 4), :]
    pl.semaphore_wait(barrier, 8 + member_count - 1 + group_count - 1)

    def remote(source, target, exchange, place, device):
        return pltpu.make_async_remote_copy(
            src_ref=source,
            dst_ref=target,
            send_sem=halo_send_sem.at[exchange, place],
            recv_sem=halo_recv_sem.at[exchange, place],
            device_id=device,
            device_id_type=MESH,
        )

    def y_copies(step):
        return [
            remote(y_send.at[step, 0, 1, pl.ds(7, 1), :], corner_recv.at[step, 0], step, 4, neighbours[4]),
            remote(y_send.at[step, 1, 1, pl.ds(0, 1), :], corner_recv.at[step, 1], step, 5, neighbours[5]),
            remote(y_send.at[step, 1, 2, pl.ds(7, 1), :], corner_recv.at[step, 2], step, 6, neighbours[6]),
            remote(y_send.at[step, 0, 2, pl.ds(0, 1), :], corner_recv.at[step, 3], step, 7, neighbours[7]),
            remote(y_send.at[step, 0], y_recv.at[step, 0], step, 2, neighbours[2]),
            remote(y_send.at[step, 1], y_recv.at[step, 1], step, 3, neighbours[3]),
        ]

    def x_copies(step):
        return [
            remote(
                streamed.at[step, pl.ds(0, 5), pl.ds(row_of(CX - 1, 0), CY), :],
                streamed.at[step, pl.ds(0, 5), pl.ds(LOW_SLAB, CY), :],
                step,
                0,
                neighbours[0],
            ),
            remote(
                streamed.at[step, pl.ds(5, 5), pl.ds(row_of(0, 0), CY), :],
                streamed.at[step, pl.ds(5, 5), pl.ds(HIGH_SLAB, CY), :],
                step,
                1,
                neighbours[1],
            ),
        ]

    def phase_copies_of(part, exchange):
        start, count = ((0, 1), (1, STEPS - 1))[part]
        steps = pl.ds(start, count)
        return [
            remote(
                phases.at[steps, 0, pl.ds(row_of(CX - 1, 0), CY), :],
                phases.at[steps, 0, pl.ds(LOW_SLAB, CY), :],
                exchange,
                0,
                neighbours[0],
            ),
            remote(
                phases.at[steps, 0, pl.ds(row_of(0, 0), CY), :],
                phases.at[steps, 0, pl.ds(HIGH_SLAB, CY), :],
                exchange,
                1,
                neighbours[1],
            ),
            remote(hy_send.at[0, steps], hy_recv.at[0, steps], exchange, 2, neighbours[2]),
            remote(hy_send.at[1, steps], hy_recv.at[1, steps], exchange, 3, neighbours[3]),
        ]

    phase_copies = [phase_copies_of(0, STEPS), phase_copies_of(1, STEPS + 2)]
    phase_copies[0] += [
        remote(
            hcorner_send.at[place], hcorner_recv.at[place], STEPS, 4 + place, neighbours[4 + place]
        )
        for place in range(4)
    ]
    halo_copies = [y_copies(step) + x_copies(step) for step in range(STEPS)]
    slab_copies = [
        remote(corner_pack.at[0], corner_pack_recv.at[0], STEPS + 1, 4, neighbours[4]),
        remote(corner_pack.at[1], corner_pack_recv.at[1], STEPS + 1, 5, neighbours[5]),
        remote(corner_pack.at[2], corner_pack_recv.at[2], STEPS + 1, 6, neighbours[6]),
        remote(corner_pack.at[3], corner_pack_recv.at[3], STEPS + 1, 7, neighbours[7]),
        remote(x_pack.at[0], x_pack_recv.at[0], STEPS + 1, 0, neighbours[0]),
        remote(x_pack.at[1], x_pack_recv.at[1], STEPS + 1, 1, neighbours[1]),
        remote(y_pack.at[0], y_pack_recv.at[0], STEPS + 1, 2, neighbours[2]),
        remote(y_pack.at[1], y_pack_recv.at[1], STEPS + 1, 3, neighbours[3]),
    ]
    for copy in halo_copies[0]:
        copy.start()
    for copy in phase_copies[0]:
        copy.start()

    for copy in slab_copies:
        copy.start()
    loads_of[4].wait()
    tile_send[...] = jnp.where(
        lane == 2 * member,
        tile_scalars[0, 0],
        jnp.where(lane == 2 * member + 1, tile_scalars[0, 1], 0),
    )
    tile_recv[member] = tile_send[...]

    def route(source, target, kind, device):
        return pltpu.make_async_remote_copy(
            src_ref=source,
            dst_ref=target,
            send_sem=route_send_sem.at[kind],
            recv_sem=route_recv_sem.at[kind],
            device_id=device,
            device_id_type=MESH,
        )

    for shift in member_shifts:
        route(tile_send, tile_recv.at[member], 0, member_device(shift)[1]).start()


    def wait_bytes(ref, semaphore):
        pltpu.make_async_copy(ref, ref, semaphore).wait()

    def update(step, prow, crow, column=None):
        final = step == STEPS - 1
        pstep, cstep = (PITCH, CY) if column is not None else (None, None)

        def rows(offset):
            if pstep is None:
                return pl.ds(prow + offset, 8)
            return pl.ds(prow + offset, 8, stride=pstep)

        cells = pl.ds(crow, 8) if cstep is None else pl.ds(crow, 8, stride=cstep)
        own = phases[step, 0, rows(0), :]
        liquid = own > -0.25
        offsets = [PITCH * direction[0] + direction[1] for direction in velocity_table]
        read, density, totals, exchanged = gather(
            own,
            [current[step, axis, cells, :] for axis in range(3)],
            lambda component: resident[step, component, cells, :],
            lambda component: streamed[step, SLOT[component], rows(-offsets[component]), :],
            lambda component: phases[
                step, version_of(velocity_table[component][2]), rows(-offsets[component]), :
            ],
            True,
        )
        interface = jnp.logical_and(liquid, own < 0.75)
        exchanged = jnp.where(interface, exchanged, 0.0)
        if step > 0:
            exchanged = exchanged + mass[step - 1, cells, :]
        if final:
            mass_out[cells, :] = exchanged
        else:
            mass[step, cells, :] = exchanged

        def put(component, value):
            value = jnp.where(liquid, value, weight_table[component])
            if final:
                pops_out[component, cells, :] = value
                return
            resident[step + 1, component, cells, :] = value
            if component == 0:
                return
            value = turned(value, velocity_table[component][2])
            streamed[step + 1, SLOT[component], rows(0), :] = value
            if column is not None:
                side, names = (0, Y_PLUS) if column > 0 else (1, Y_MINUS)
                if component in names:
                    y_send[step + 1, side, names.index(component)] = value

        relax(read, density, totals, put)
        if not final:
            for axis, value in enumerate(momentum_after(totals)):
                current[step + 1, axis, cells, :] = jnp.where(liquid, value, 0.0)

    def interior(step):
        def slab(x, carry):
            for y in (1, 7):
                update(step, PITCH * x + PITCH + 8 + y, CY * x + y)
            return carry

        loop(1, CX - 1, slab, 1)

    def y_border(step):
        for y in (0, CY - 1):
            update(step, row_of(0, y), y, column=y)

    def x_border(step):
        def slab(index, carry):
            x = (CX - 1) * (index // 2)
            half = 8 * remainder(index, 2)
            update(
                step,
                aligned(PITCH * x + PITCH + 8 + half, 8),
                aligned(CY * x + half, 8),
            )
            return carry

        loop(0, 4, slab, 4)

    corners = (
        (7, row_of(-1, -1), CX - 1),
        (8, row_of(CX, CY), 0),
        (9, row_of(-1, CY), CX - 1),
        (10, row_of(CX, -1), 0),
    )

    def unpack(step):
        for copy in halo_copies[step]:
            copy.wait_recv()
        for side, (y, names) in enumerate(((-1, Y_PLUS), (CY, Y_MINUS))):
            for place, component in enumerate(names):
                streamed[step, SLOT[component], pl.ds(row_of(0, y), CX, stride=PITCH), :] = y_recv[
                    step, side, place
                ]
        for place, (component, row, x) in enumerate(corners):
            streamed[step, SLOT[component], pl.ds(row, 1), :] = corner_recv[step, place]

    def unpack_phases(part):
        for copy in phase_copies[part]:
            copy.wait_recv()
        at_west, at_east = gx == 0, gx == gx_count - 1
        at_south, at_north = gy == 0, gy == gy_count - 1

        def one(step, carry):
            for start, edge in ((LOW_SLAB, at_west), (HIGH_SLAB, at_east)):
                for half in (0, 8):
                    rows = pl.ds(start + half, 8)
                    put_phase(step, rows, jnp.where(edge, GAS, phases[step, 0, rows, :]))
            for side, (y, edge) in enumerate(((-1, at_south), (CY, at_north))):
                rows = pl.ds(row_of(0, y), CX, stride=PITCH)
                put_phase(step, rows, jnp.where(edge, GAS, hy_recv[side, step]))
            edges = (
                at_west | at_south,
                at_east | at_north,
                at_west | at_north,
                at_east | at_south,
            )
            for place, (component, row, x) in enumerate(corners):
                code = hcorner_recv[place, pl.ds(step, 1), :]
                phases[step, 0, pl.ds(row, 1), :] = jnp.where(edges[place], GAS, code)
            return carry

        loop(*((0, 1), (1, STEPS))[part], one, STEPS)

    def find_tiles():
        wait_bytes(tile_recv.at[pl.ds(0, member_count - 1)], route_recv_sem.at[0])
        names = tile_recv[0]
        for place in range(1, member_count):
            names = names + tile_recv[place]
        sublane = lax.broadcasted_iota(jnp.int32, (8, NZ), 0)
        none = 2 * member_count
        lasts = earlies = jnp.zeros((8, NZ), jnp.int32)
        for place in range(group_count):
            owner_x, owner_y = device_of(place // Y_COUNT, place % Y_COUNT, sublane, core)
            wanted = owner_x * gy_count + owner_y
            match = jnp.logical_and(names == wanted, lane < none)
            last = jnp.max(jnp.where(match, lane, -1), axis=1, keepdims=True)
            early = jnp.min(jnp.where(match, lane, none), axis=1, keepdims=True)
            early = jnp.where(early == last, none, early)
            last = jnp.where(last < 0, none, last)
            lasts = jnp.where(lane == place, last, lasts)
            earlies = jnp.where(lane == place, early, earlies)
        index_block[0] = lasts
        index_block[1] = earlies
        copy = pltpu.make_async_copy(index_block, index_scalars, local_sem.at[4])
        copy.start()
        copy.wait()

    def widen_weights():
        loads_of[3].wait()
        for part in range(CELLS // 16):
            rows = pl.ds(16 * part, 16)
            weights[rows, :] = weights_packed[rows, :].astype(F32)

    def unpack_slab():
        for copy in slab_copies:
            copy.wait_recv()

        def fields(part, carry):
            quarter = pl.ds(4 * remainder(part, 2), 4)
            for j in range(4):
                field = 4 * part + j
                for half in (0, 8):
                    rows = pl.ds(WIDE + half, 8)
                    low = rolled(x_pack_recv[0, part, pl.ds(half, 8), :], -32 * j)
                    high = rolled(x_pack_recv[1, part, pl.ds(half, 8), :], 96 - 32 * j)
                    slab[field, rows, :] = jnp.where(
                        lane < 32, low, jnp.where(lane >= 96, high, slab[field, rows, :])
                    )
                for side, row, west_corner, east_corner in ((0, 0, 0, 3), (1, CY + WIDE, 2, 1)):
                    middle = rolled(
                        y_pack_recv[side, part, pl.ds(4 * (j // 2), 4), :], 32 - 64 * (j % 2)
                    )
                    low = rolled(corner_pack_recv[west_corner, part // 2, quarter, :], -32 * j)
                    high = rolled(corner_pack_recv[east_corner, part // 2, quarter, :], 96 - 32 * j)
                    slab[field, pl.ds(row, 4), :] = jnp.where(
                        lane4 < 32, low, jnp.where(lane4 >= 96, high, middle)
                    )
            return carry

        loop(0, FIELDS // 4, fields, 6)
        low_lane = jnp.where(gx == 0, DEEP * WIDE, 0)
        high_lane = jnp.where(gx == gx_count - 1, NZ - DEEP * WIDE, NZ)
        low_row = jnp.where(gy == 0, WIDE, 0)
        high_row = jnp.where(gy == gy_count - 1, CY + WIDE, SLAB_ROWS)
        level = lax.rem(lane, DEEP)

        def ready(block, carry):
            start = aligned(8 * block, 8)
            cells = pl.ds(start, 8)
            rows = pl.ds(aligned(start + 8, 8), 8)
            totals = [None, None, None]
            for component in range(1, 19, 2):
                direction = velocity_table[component]
                along = slab[component, cells, :]
                against = slab[component + 1, cells, :]
                add_momentum(totals, direction, along - against)
                shift = slab_shift(direction)
                slab_streamed[0, SLOT[component], rows, :] = rolled(along, shift)
                slab_streamed[0, SLOT[component + 1], rows, :] = rolled(against, -shift)
            for axis in range(3):
                slab_current[0, axis, cells, :] = totals[axis]
            row = lax.broadcasted_iota(jnp.int32, (8, NZ), 0) + start
            inside = jnp.logical_and(
                jnp.logical_and(lane >= low_lane, lane < high_lane),
                jnp.logical_and(row >= low_row, row < high_row),
            )
            for step in range(STEPS):
                code = jnp.where(inside, slab[19 + step, cells, :], GAS)
                for shift_x in (-1, 0, 1):
                    for shift_z in (-1, 0, 1):
                        direction = (shift_x, 0, shift_z)
                        value = rolled(code, slab_shift(direction))
                        if shift_z == 1:
                            value = jnp.where(level == 0, WALL, value)
                        slab_phases[step, slab_version(direction), rows, :] = value
            return carry

        loop(0, SLAB_ROWS // 8, ready, 3)

    def slab_update(step, start):
        cells = pl.ds(start, 8)

        def rows(offset):
            return pl.ds(start + 8 + offset, 8)

        def own_of(component):
            if step == 0:
                return slab[component, cells, :]
            return slab_resident[step - 1, component, cells, :]

        own = slab_phases[step, slab_version((0, 0, 0)), rows(0), :]
        liquid = own > -0.25
        read, density, totals, _ = gather(
            own,
            [slab_current[step, axis, cells, :] for axis in range(3)],
            own_of,
            lambda component: slab_streamed[
                step, SLOT[component], rows(-velocity_table[component][1]), :
            ],
            lambda component: slab_phases[
                step,
                slab_version(velocity_table[component]),
                rows(-velocity_table[component][1]),
                :,
            ],
            False,
        )
        slab_deck[step, cells, :] = jnp.where(liquid, density * (1.0 / 3.0), 0.0)
        if step == STEPS - 1:
            return

        def put(component, value):
            value = jnp.where(liquid, value, weight_table[component])
            slab_resident[step, component, cells, :] = value
            if component > 0:
                slab_streamed[step + 1, SLOT[component], rows(0), :] = rolled(
                    value, slab_shift(velocity_table[component])
                )

        relax(read, density, totals, put)
        for axis, value in enumerate(momentum_after(totals)):
            slab_current[step + 1, axis, cells, :] = jnp.where(liquid, value, 0.0)

    def slab_steps():
        for step in range(STEPS - 1):

            def block(index, carry, step=step):
                slab_update(step, aligned(8 * index, 8))
                return carry

            loop(0, SLAB_ROWS // 8, block, 3)
        for start in (WIDE, WIDE + 8):
            slab_update(STEPS - 1, start)

    def first_leg():
        def one(step, carry):
            for tile in range(2):
                sums = [None] * 8
                for part in range(8):
                    x = 4 * tile + part // 2
                    cells = pl.ds(64 * tile + 8 * part, 8)
                    pressure = slab_deck[step, pl.ds(WIDE + 8 * (part % 2), 8), :]
                    pressure = pressure.astype(jnp.bfloat16).astype(F32)
                    place = DEEP * (x + WIDE)
                    pressure = jnp.broadcast_to(pressure[:, place : place + 1], (8, NZ))
                    for column in range(8):
                        term = pressure * weights[cells, pl.ds(NZ * column, NZ)]
                        sums[column] = term if part == 0 else sums[column] + term
                for column in range(8):
                    partial[column, tile, pl.ds(step, 1), :] = jnp.sum(
                        sums[column], axis=0, keepdims=True
                    )
            return carry

        loop(0, STEPS, one, 2)
        for tile in range(2):
            first[2 * member + tile] = partial[chip_z, tile]

        for shift in member_shifts:
            other_z, device = member_device(shift)
            route(partial.at[other_z], first.at[pl.ds(2 * member, 2)], 1, device).start()

    def second_leg():
        wait_bytes(first.at[pl.ds(0, 2 * (member_count - 1))], route_recv_sem.at[1])

        def owners(place, carry):
            for z in range(Z_COUNT):
                second_send[place, z] = (
                    first[index_scalars[0, z, place]] + first[index_scalars[1, z, place]]
                )
            return carry

        loop(0, group_count, owners, 4)
        second_recv[group] = second_send[group]

        for shift in group_shifts:
            other, device = group_device(shift)
            route(second_send.at[other], second_recv.at[group], 2, device).start()

    def third_leg():
        wait_bytes(second_recv.at[pl.ds(0, group_count - 1)], route_recv_sem.at[2])
        for z in range(Z_COUNT):
            total = second_recv[0, z]
            for place in range(1, group_count):
                total = total + second_recv[place, z]
            third_send[z] = total
        third_recv[chip_z] = third_send[chip_z]
        for shift in z_shifts:
            other_z, device = member_device((shift, 0))
            route(third_send.at[other_z], third_recv.at[chip_z], 3, device).start()

    def collect():
        wait_bytes(third_recv.at[pl.ds(0, Z_COUNT - 1)], route_recv_sem.at[3])
        for z in range(Z_COUNT):
            loads_out[:, pl.ds(NZ * z, NZ)] = third_recv[z]

    first[2 * member_count] = jnp.zeros((STEPS, NZ), F32)

    for step in range(STEPS):
        if step == 0:
            widen_weights()
            interior(step)
            unpack_phases(0)
            for copy in phase_copies[1]:
                copy.start()
        if step == 1:
            unpack_slab()
            slab_steps()
            first_leg()
            interior(step)
            unpack_phases(1)
            find_tiles()
        if step == 2:
            interior(step)
            second_leg()
        if step == 3:
            interior(step)
            third_leg()
        unpack(step)
        y_border(step)
        if step < STEPS - 1:
            for copy in halo_copies[step + 1][:6]:
                copy.start()
        x_border(step)
        if step < STEPS - 1:
            for copy in halo_copies[step + 1][6:]:
                copy.start()

    collect()
    for copies in phase_copies:
        for copy in copies:
            copy.wait_send()
    for copy in slab_copies:
        copy.wait_send()
    for copies in halo_copies:
        for copy in copies:
            copy.wait_send()
    wait_bytes(tile_recv.at[pl.ds(0, member_count - 1)], route_send_sem.at[0])
    wait_bytes(first.at[pl.ds(0, 2 * (member_count - 1))], route_send_sem.at[1])
    wait_bytes(second_send.at[pl.ds(0, group_count - 1)], route_send_sem.at[2])
    wait_bytes(third_send.at[pl.ds(0, Z_COUNT - 1)], route_send_sem.at[3])


def hand_over(pops, mass, loads, pops_out, mass_out, loads_out, semaphores):
    copies = [
        pltpu.make_async_copy(pops, pops_out, semaphores.at[0]),
        pltpu.make_async_copy(mass, mass_out, semaphores.at[1]),
        pltpu.make_async_copy(loads, loads_out, semaphores.at[2]),
    ]
    for copy in copies:
        copy.start()
    for copy in copies:
        copy.wait()


def per_device(gx_count, gy_count, populations, cell_flags, fill_level, tile_block, deck_weights):
    members, groups = 2 * Z_COUNT, Y_COUNT * (gx_count // (2 * Z_HIGH))
    whole = pl.BlockSpec(memory_space=pltpu.HBM)
    keep = pl.BlockSpec(memory_space=pl.ANY)
    placed = functools.partial(pltpu.with_memory_space_constraint, memory_space=pltpu.HBM)
    pops, mass, loads = pl.pallas_call(
        functools.partial(kernel, gx_count, gy_count),
        out_shape=(
            pltpu.VMEM((19, CELLS, NZ), F32),
            pltpu.VMEM((CELLS, NZ), F32),
            pltpu.VMEM((STEPS, 1024), F32),
        ),
        in_specs=[whole] * 5,
        out_specs=(pl.BlockSpec(memory_space=pltpu.VMEM),) * 3,
        scratch_shapes=[
            pltpu.VMEM((STEPS, 18, ROWS, NZ), F32),
            pltpu.VMEM((STEPS, 19, CELLS, NZ), F32),
            pltpu.VMEM((STEPS, 3, ROWS, NZ), F32),
            pltpu.VMEM((STEPS, 3, CELLS, NZ), F32),
            pltpu.VMEM((STEPS - 1, CELLS, NZ), F32),
            pltpu.VMEM((STEPS, CELLS, NZ), jnp.int32),
            pltpu.VMEM((CELLS, NZ), F32),
            pltpu.VMEM((CELLS, 1024), jnp.bfloat16),
            pltpu.VMEM((CELLS, 1024), F32),
            pltpu.VMEM((STEPS, 2, 5, 8, NZ), F32),
            pltpu.VMEM((STEPS, 2, 5, 8, NZ), F32),
            pltpu.VMEM((STEPS, 4, 1, NZ), F32),
            pltpu.VMEM((2, STEPS, 8, NZ), F32),
            pltpu.VMEM((2, STEPS, 8, NZ), F32),
            pltpu.VMEM((4, STEPS, NZ), F32),
            pltpu.VMEM((4, STEPS, NZ), F32),
            pltpu.VMEM((8, NZ), jnp.int32),
            pltpu.VMEM((members, 8, NZ), jnp.int32),
            pltpu.VMEM((2, 8, NZ), jnp.int32),
            pltpu.SMEM((2, 8, NZ), jnp.int32),
            pltpu.VMEM((FIELDS, SLAB_ROWS, NZ), F32),
            pltpu.VMEM((STEPS - 1, 19, SLAB_ROWS, NZ), F32),
            pltpu.VMEM((STEPS, 18, SLAB_ROWS + 16, NZ), F32),
            pltpu.VMEM((STEPS, 9, SLAB_ROWS + 16, NZ), F32),
            pltpu.VMEM((STEPS, 3, SLAB_ROWS, NZ), F32),
            pltpu.VMEM((STEPS, SLAB_ROWS, NZ), F32),
            pltpu.VMEM((2, FIELDS // 4, CY, NZ), F32),
            pltpu.VMEM((2, FIELDS // 4, 8, NZ), F32),
            pltpu.VMEM((4, FIELDS // 8, 8, NZ), F32),
            pltpu.VMEM((2, FIELDS // 4, CY, NZ), F32),
            pltpu.VMEM((2, FIELDS // 4, 8, NZ), F32),
            pltpu.VMEM((4, FIELDS // 8, 8, NZ), F32),
            pltpu.SMEM((1, 2), jnp.int32),
            pltpu.VMEM((8, 2, STEPS, NZ), F32),
            pltpu.VMEM((2 * members + 1, STEPS, NZ), F32),
            pltpu.VMEM((groups, Z_COUNT, STEPS, NZ), F32),
            pltpu.VMEM((groups, Z_COUNT, STEPS, NZ), F32),
            pltpu.VMEM((Z_COUNT, STEPS, NZ), F32),
            pltpu.VMEM((Z_COUNT, STEPS, NZ), F32),
            pltpu.SemaphoreType.DMA((9,)),
            pltpu.SemaphoreType.DMA((STEPS + 3, 8)),
            pltpu.SemaphoreType.DMA((STEPS + 3, 8)),
            pltpu.SemaphoreType.DMA((4,)),
            pltpu.SemaphoreType.DMA((4,)),
        ],
        compiler_params=pltpu.CompilerParams(
            collective_id=0, has_side_effects=True, vmem_limit_bytes=32 * 1024 * 1024
        ),
    )(
        placed(populations.reshape(19, CELLS, NZ)),
        placed(cell_flags.reshape(STEPS, CELLS, NZ)),
        placed(fill_level.reshape(CELLS, NZ)),
        placed(tile_block.reshape(1, 2)),
        placed(deck_weights.reshape(CELLS, 1024)),
    )
    pops, mass, loads = pl.pallas_call(
        hand_over,
        out_shape=(
            pltpu.HBM((19, CELLS, NZ), F32),
            pltpu.HBM((CELLS, NZ), F32),
            pltpu.HBM((STEPS, 1024), F32),
        ),
        in_specs=[keep] * 3,
        out_specs=(whole, whole, whole),
        scratch_shapes=[pltpu.SemaphoreType.DMA((3,))],
    )(*(pltpu.with_memory_space_constraint(part, pltpu.VMEM) for part in (pops, mass, loads)))
    return (
        pops.reshape(19, CX, CY, NZ),
        mass.reshape(CX, CY, NZ),
        loads.reshape(1, STEPS, 1024),
    )


def solution(mesh):
    placed = (
        P(None, "gx", "gy", None),
        P(None, "gx", "gy", None),
        P("gx", "gy", None),
        P("gx", "gy"),
        P("gx", "gy", None, None),
    )
    return jax.shard_map(
        functools.partial(per_device, mesh.shape["gx"], mesh.shape["gy"]),
        mesh=mesh,
        in_specs=placed,
        out_specs=(P(None, "gx", "gy", None), P("gx", "gy", None), P(("gx", "gy"), None, None)),
        check_vma=False,
    )
```
